512 devices in a mesh: aperture: 64 (over y_hi, z, core), range: 8 (over y_lo, x).
Axes of the slice: x: 4, y: 8 (y_hi: 4, y_lo: 2; y = y_hi * 2 + y_lo), z: 8, core: 2. Of those that a mesh axis runs over, the one named last changes fastest.
Arguments:
- echoes: bfloat16 [2, 2048, 8192], P(None, 'aperture', 'range'), may hold values from -6 to 6
- transmit_chirp: bfloat16 [2, 512], replicated, may hold values from -0.1875 to 0.1875
- band_weights: float32 [4, 2, 2, 2048, 16], P(None, None, None, 'aperture'), may hold values from -0.75 to 0.75
- band_offsets: int32 [4, 2, 2048], P(None, None, 'aperture'), may hold values from -16 to 16
- band_widths: int32 [4, 2, 2048], P(None, None, 'aperture'), may hold values from 8 to 16
- child_rows: int32 [4, 2048], P(None, 'aperture'), may hold values from 0 to 15
Outputs:
- subimage: bfloat16 [2, 2048, 8192], P(None, 'aperture', 'range')
The draws below stay inside these ranges and needn't reach their ends.
All inputs are finite; a program needn't handle non-finite values.
Results may differ from the reference program's by a relative error of at most 0.007.
Values may be sent and summed in bfloat16 or wider, within the bound.
No kernel may reach another device: no remote copies, remote signals or barrier semaphores. Data moves between devices by JAX's collectives and lax.ppermute only.
A program may use at most 128 MiB of HBM per device.

```python
import jax
import jax.numpy as jnp
from jax import lax

RANGE = 8192
P_DEV = 32
TAPS = 512
KERN = 16
SHIFT = 16
LEVELS = 4
PULSES = 2048
HALF = 16
N_APERTURE = 64


def with_ends(values, key, low, high):
    place = [jax.random.randint(jax.random.fold_in(key, axis), (), 0, length) for axis, length in enumerate(values.shape)]
    main_axis = values.shape.index(max(values.shape))
    neighbour = place[:main_axis] + [(place[main_axis] + 1) % values.shape[main_axis]] + place[main_axis + 1:]
    return values.at[tuple(place)].set(low).at[tuple(neighbour)].set(high)


def level_of(stream_key, dims, pieces, low, top_value):
    def one(dim, shards_of):
        draws = jax.random.uniform(jax.random.fold_in(jax.random.fold_in(stream_key, 6), dim), (shards_of,), jnp.float32, low / len(pieces), top_value / len(pieces))
        return jnp.repeat(jnp.exp(draws), dims[dim] // shards_of).reshape((-1,) + (1,) * (len(dims) - dim - 1))

    level = one(*pieces[0])
    for cut in pieces[1:]:
        level = level * one(*cut)
    return level


def bell_draw(stream_key, shape, scale, reach, split=(), held_as=jnp.bfloat16):
    drawn = scale * jax.random.normal(stream_key, shape, jnp.float32)
    if split:
        drawn = drawn * level_of(stream_key, shape, split, -0.22, 0.18)
    return jnp.clip(drawn, -reach, reach).astype(held_as)


def setup_inputs(seed: int = 0) -> dict:
    arg_keys = jax.random.split(jax.random.key(seed), 7)
    return {
        "echoes": bell_draw(arg_keys[0], (2, PULSES, RANGE), 1.0, 6.0, ((1, 64), (2, 8))),
        "transmit_chirp": bell_draw(arg_keys[1], (2, TAPS), (2 * TAPS) ** -0.5, 0.1875),
        "band_weights": bell_draw(arg_keys[2], (LEVELS, 2, 2, PULSES, KERN), (4 * KERN) ** -0.5, 0.75, ((3, 64),), jnp.float32),
        "band_offsets": with_ends(jax.random.randint(arg_keys[3], (LEVELS, 2, PULSES), 0 - SHIFT, SHIFT + 1), jax.random.fold_in(arg_keys[3], 1), 0 - SHIFT, SHIFT).astype(jnp.int32),
        "band_widths": with_ends(jax.random.randint(arg_keys[4], (LEVELS, 2, PULSES), KERN // 2, KERN + 1), jax.random.fold_in(arg_keys[4], 1), KERN // 2, KERN).astype(jnp.int32),
        "child_rows": with_ends(jax.random.randint(arg_keys[5], (LEVELS, PULSES), 0, HALF), jax.random.fold_in(arg_keys[5], 1), 0, HALF - 1).astype(jnp.int32),
    }


def compress(padded, transmit_chirp, out_length):
    chirp_values = transmit_chirp.astype(jnp.float32)
    chirp_real = chirp_values[0]
    chirp_imag = chirp_values[1]
    kernel = jnp.stack([jnp.stack([chirp_real, chirp_imag]), jnp.stack([-chirp_imag, chirp_real])])
    result = lax.conv_general_dilated(padded.astype(jnp.float32), kernel, (1,), "VALID",
                                      dimension_numbers=("CNW", "OIW", "CNW"),
                                      precision=lax.Precision.HIGHEST)
    return result[:, :, :out_length]


def shifted_sum(source, kernel, offsets_now, widths_now, child_index, margin, out_length):
    kern_taps = kernel.shape[-1]
    rows_in = source[:, child_index, :]
    starts = (offsets_now + margin - kern_taps // 2).astype(jnp.int32)

    def cut_window(single_row, start_bin):
        return lax.dynamic_slice_in_dim(single_row, start_bin, out_length + kern_taps - 1, 1)

    windows = jax.vmap(cut_window, in_axes=(1, 0), out_axes=1)(rows_in, starts)
    live_taps = (jnp.arange(kern_taps, dtype=jnp.int32)[None, :] < widths_now[:, None]).astype(jnp.float32)
    weights = kernel * live_taps[None]
    real_part = jnp.zeros((windows.shape[1], out_length), jnp.float32)
    imag_part = jnp.zeros((windows.shape[1], out_length), jnp.float32)
    for tap_index in range(kern_taps):
        shifted = windows[:, :, tap_index:tap_index + out_length].astype(jnp.float32)
        weight_real = weights[0, :, tap_index:tap_index + 1]
        weight_imag = weights[1, :, tap_index:tap_index + 1]
        real_part = real_part + weight_real * shifted[0] - weight_imag * shifted[1]
        imag_part = imag_part + weight_real * shifted[1] + weight_imag * shifted[0]
    return jnp.stack([real_part, imag_part])


def merge_rows(lower_child, upper_child, kernel, offsets_now, widths_now, child_index, margin, out_length):
    lower_term = shifted_sum(lower_child, kernel[0], offsets_now[0], widths_now[0], child_index, margin, out_length)
    upper_term = shifted_sum(upper_child, kernel[1], offsets_now[1], widths_now[1], child_index, margin, out_length)
    return lower_term + upper_term


def reference(echoes, transmit_chirp, band_weights, band_offsets, band_widths, child_rows):
    padded = jnp.pad(echoes, ((0, 0), (0, 0), (TAPS // 2, TAPS // 2)))
    blocks = padded.reshape(2, N_APERTURE, P_DEV, RANGE + TAPS).transpose(1, 0, 2, 3)
    compressed = lax.map(lambda block: compress(block, transmit_chirp, RANGE).astype(jnp.bfloat16), blocks)
    subimage = compressed
    margin = SHIFT + KERN // 2
    for level_index in range(LEVELS):
        padded_level = jnp.pad(subimage, ((0, 0), (0, 0), (0, 0), (margin, margin)))

        def one_device(device):
            side_bit = (device >> level_index) & 1
            lower_device = device - side_bit * (1 << level_index)
            upper_device = lower_device + (1 << level_index)
            lower_block = lax.dynamic_index_in_dim(padded_level, lower_device, 0, False)
            upper_block = lax.dynamic_index_in_dim(padded_level, upper_device, 0, False)
            lower_child = lax.dynamic_slice_in_dim(lower_block, side_bit * HALF, HALF, 1)
            upper_child = lax.dynamic_slice_in_dim(upper_block, side_bit * HALF, HALF, 1)
            kernel = lax.dynamic_slice_in_dim(band_weights[level_index], device * P_DEV, P_DEV, 2)
            offsets_now = lax.dynamic_slice_in_dim(band_offsets[level_index], device * P_DEV, P_DEV, 1)
            widths_now = lax.dynamic_slice_in_dim(band_widths[level_index], device * P_DEV, P_DEV, 1)
            child_index = lax.dynamic_slice_in_dim(child_rows[level_index], device * P_DEV, P_DEV, 0)
            merged = merge_rows(lower_child, upper_child, kernel, offsets_now, widths_now, child_index, margin, RANGE)
            return merged.astype(jnp.bfloat16)

        subimage = lax.map(one_device, jnp.arange(N_APERTURE, dtype=jnp.int32))
    return subimage.transpose(1, 0, 2, 3).reshape(2, PULSES, RANGE)
```

```python
import jax
import jax.numpy as jnp
from jax import lax
from jax.experimental import pallas as pl
from jax.experimental.pallas import tpu as pltpu
from jax.sharding import PartitionSpec as P

KERN = 16
SHIFT = 16
LEVELS = 4
TAPS = 512
HALF = 16
ROWS = 32
LANES = 128
BINS = 1024
RIM = 128
FRAME = BINS + 2 * RIM
HALO = RIM + TAPS // 2
SPAN = LANES + TAPS
COARSE = 6
FINE = 8
COLS = COARSE * 64
VMEM = 48 * 1024 * 1024


def column(row):
    lane = lax.broadcasted_iota(jnp.int32, (ROWS, ROWS), 1)
    sub = lax.broadcasted_iota(jnp.int32, (ROWS, ROWS), 0)
    wide = jnp.broadcast_to(row.astype(jnp.float32), (ROWS, ROWS))
    return jnp.sum(jnp.where(lane == sub, wide, 0.0), axis=1, keepdims=True)


def prepare_kernel(place, chirp, weights, offsets, widths, child, toeplitz, bank):
    device = place[0]

    taps = chirp[...].astype(jnp.float32)
    taps = jnp.concatenate([taps, jnp.zeros((2, SPAN - TAPS), jnp.float32)], axis=1)
    real = pltpu.roll(jnp.broadcast_to(taps[0:1], (LANES, SPAN)), 0, 1, stride=1, stride_axis=0)
    imag = pltpu.roll(jnp.broadcast_to(taps[1:2], (LANES, SPAN)), 0, 1, stride=1, stride_axis=0)
    toeplitz[0:LANES, 0:SPAN] = real.astype(jnp.bfloat16)
    toeplitz[0:LANES, SPAN : 2 * SPAN] = imag.astype(jnp.bfloat16)
    toeplitz[LANES : 2 * LANES, 0:SPAN] = (-imag).astype(jnp.bfloat16)
    toeplitz[LANES : 2 * LANES, SPAN : 2 * SPAN] = real.astype(jnp.bfloat16)

    lane = lax.broadcasted_iota(jnp.int32, (ROWS, LANES), 1)
    upper = lane >= 64
    shift_of = (lane & 63).astype(jnp.float32)
    col = lax.broadcasted_iota(jnp.int32, (256, COLS), 1)
    row = lax.broadcasted_iota(jnp.int32, (256, COLS), 0)
    wanted = row - (((col >> 4) & 3) * 64 + (col >> 6) * 8)
    child_of = (lax.broadcasted_iota(jnp.int32, (HALF, COLS), 1) & 15).astype(jnp.float32)

    stacks = []
    masks = []
    for level in range(LEVELS):
        side = (device >> level) & 1
        if level + 1 < LEVELS:
            first = ((device >> (level + 1)) & 1) == 1
        else:
            first = None

        def order(pair):
            if first is None:
                return pair
            low, high = pair[0:HALF], pair[HALF:ROWS]
            return jnp.concatenate(
                [jnp.where(first, high, low), jnp.where(first, low, high)], axis=0
            )

        spread = []
        for which in range(2):
            t = side if which == 0 else 1 - side
            offset = column(offsets[level, pl.ds(t, 1), :])
            width = column(widths[level, pl.ds(t, 1), :])
            wr = weights[level, t, 0]
            wi = weights[level, t, 1]
            tap = shift_of - (offset + float(SHIFT))
            tap = jnp.where(tap < width, tap, -1.0)
            total = jnp.zeros((ROWS, LANES), jnp.float32)
            for k in range(KERN):
                both = jnp.where(upper, wi[:, k : k + 1], wr[:, k : k + 1])
                total = jnp.where(tap == float(k), both, total)
            spread.append(total)
        to_real = order(
            jnp.concatenate([jnp.where(upper, -s, s) for s in spread], axis=1)
        )
        to_imag = order(jnp.concatenate([pltpu.roll(s, 64, 1) for s in spread], axis=1))
        both = jnp.concatenate([to_real, to_imag], axis=0)
        high = both.astype(jnp.bfloat16)
        low = (both - high.astype(jnp.float32)).astype(jnp.bfloat16)
        stacks += [high, low]
        chosen = order(jnp.broadcast_to(column(child[pl.ds(level, 1), :]), (ROWS, COLS)))
        mask = jnp.concatenate([chosen[0:HALF] == child_of, chosen[HALF:ROWS] == child_of], axis=0)
        masks.append(jnp.concatenate([mask, mask], axis=0))
    stack = jnp.concatenate(stacks, axis=0)
    for b in range(FINE):
        pick = (wanted == b).astype(jnp.float32).astype(jnp.bfloat16)
        out = jnp.dot(stack, pick, preferred_element_type=jnp.float32)
        for level in range(LEVELS):
            for part in range(2):
                piece = out[(level * 2 + part) * 64 : (level * 2 + part + 1) * 64]
                piece = jnp.where(masks[level], piece, 0.0).astype(jnp.bfloat16)
                bank[level, b * 64 : (b + 1) * 64, part * COLS : (part + 1) * COLS] = piece


def inside_mask(place, rows):
    position = place[1] * BINS - RIM
    bins = lax.broadcasted_iota(jnp.int32, (rows, FRAME), 1) + position
    return (bins >= 0) & (bins < place[2])


def compress_kernel(place, echoes, left, right, toeplitz, kept, sent, window):
    start = pl.multiple_of((place[0] & 1) * HALF, HALF)
    other = pl.multiple_of((1 - (place[0] & 1)) * HALF, HALF)
    blocks = FRAME // LANES
    tiles = SPAN // LANES
    first = HALO // LANES
    last = first + BINS // LANES
    for part in range(2):
        for half, at in enumerate((start, other)):
            for tile in range(blocks + tiles - 1):
                if tile < first:
                    piece = left[part, pl.ds(at, HALF), tile * LANES : (tile + 1) * LANES]
                elif tile < last:
                    spot = (tile - first) * LANES
                    piece = echoes[part, pl.ds(at, HALF), spot : spot + LANES]
                else:
                    spot = (tile - last) * LANES
                    piece = right[part, pl.ds(at, HALF), spot : spot + LANES]
                for block in range(max(0, tile - tiles + 1), min(blocks, tile + 1)):
                    spot = part * SPAN + (tile - block) * LANES
                    top = block * ROWS + half * HALF
                    window[top : top + HALF, spot : spot + LANES] = piece
    result = lax.dot_general(
        window[...], toeplitz[...], (((1,), (1,)), ((), ())), preferred_element_type=jnp.float32
    )
    position = place[1] * BINS - RIM
    for block in range(blocks):
        bins = lax.broadcasted_iota(jnp.int32, (ROWS, 2 * LANES), 1) & (LANES - 1)
        bins = bins + (position + block * LANES)
        inside = (bins >= 0) & (bins < place[2])
        piece = jnp.where(inside, result[block * ROWS : (block + 1) * ROWS], 0.0)
        piece = piece.astype(jnp.bfloat16)
        at = slice(block * LANES, (block + 1) * LANES)
        for part in range(2):
            lanes = slice(part * LANES, (part + 1) * LANES)
            kept[part * HALF : (part + 1) * HALF, at] = piece[0:HALF, lanes]
            sent[part * HALF : (part + 1) * HALF, at] = piece[HALF:ROWS, lanes]


def merged_beams(place, mine, theirs, bank, stack):
    source = jnp.concatenate([mine[...], theirs[...]], axis=0).astype(jnp.float32)
    for a in range(COARSE):
        shift = (24 - 8 * a) % FRAME
        moved = pltpu.roll(source, shift, 1) if shift else source
        moved = moved.astype(jnp.bfloat16)
        stack[a * 64 : (a + 1) * 64] = moved
        stack[COLS + a * 64 : COLS + (a + 1) * 64] = moved
    total = None
    product = jnp.dot(bank[0], stack[...], preferred_element_type=jnp.float32)
    for b in range(FINE):
        piece = product[b * 64 : (b + 1) * 64]
        if b:
            piece = pltpu.roll(piece, FRAME - b, 1)
        total = piece if total is None else total + piece
    return total


def level_kernel(place, mine, theirs, bank, kept, sent, stack):
    total = merged_beams(place, mine, theirs, bank, stack)
    total = jnp.where(inside_mask(place, 64), total, 0.0).astype(jnp.bfloat16)
    for part in range(2):
        kept[part * HALF : (part + 1) * HALF] = total[part * ROWS : part * ROWS + HALF]
        sent[part * HALF : (part + 1) * HALF] = total[part * ROWS + HALF : (part + 1) * ROWS]


def last_kernel(place, mine, theirs, bank, out, stack):
    total = merged_beams(place, mine, theirs, bank, stack)[:, RIM : RIM + BINS].astype(jnp.bfloat16)
    out[0] = total[0:ROWS]
    out[1] = total[ROWS : 2 * ROWS]


WHOLE = pl.BlockSpec(memory_space=pltpu.VMEM)
SCALARS = pl.BlockSpec(memory_space=pltpu.SMEM)
PARAMS = pltpu.CompilerParams(vmem_limit_bytes=VMEM)


def prepare(place, chirp, weights, offsets, widths, child):
    return pl.pallas_call(
        prepare_kernel,
        out_shape=(
            jax.ShapeDtypeStruct((2 * LANES, 2 * SPAN), jnp.bfloat16),
            jax.ShapeDtypeStruct((LEVELS, FINE * 64, 2 * COLS), jnp.bfloat16),
        ),
        in_specs=[SCALARS] + [WHOLE] * 5,
        out_specs=(WHOLE, WHOLE),
        compiler_params=PARAMS,
        cost_estimate=pl.CostEstimate(flops=4_000_000_000, bytes_accessed=4_000_000, transcendentals=0),
        name="prepare",
    )(place, chirp, weights, offsets, widths, child)


def compress(place, echoes, left, right, toeplitz):
    half = jax.ShapeDtypeStruct((2 * HALF, FRAME), jnp.bfloat16)
    return pl.pallas_call(
        compress_kernel,
        out_shape=(half, half),
        in_specs=[SCALARS] + [WHOLE] * 4,
        out_specs=(WHOLE, WHOLE),
        scratch_shapes=[pltpu.VMEM((FRAME // LANES * ROWS, 2 * SPAN), jnp.bfloat16)],
        compiler_params=PARAMS,
        name="compress",
    )(place, echoes, left, right, toeplitz)


def merge(place, mine, theirs, bank, level):
    half = jax.ShapeDtypeStruct((2 * HALF, FRAME), jnp.bfloat16)
    last = level + 1 == LEVELS
    return pl.pallas_call(
        last_kernel if last else level_kernel,
        grid=(1,),
        out_shape=jax.ShapeDtypeStruct((2, ROWS, BINS), jnp.bfloat16) if last else (half, half),
        in_specs=[
            SCALARS,
            WHOLE,
            WHOLE,
            pl.BlockSpec((1, FINE * 64, 2 * COLS), lambda i: (level, 0, 0)),
        ],
        out_specs=WHOLE if last else (WHOLE, WHOLE),
        scratch_shapes=[pltpu.VMEM((2 * COLS, FRAME), jnp.bfloat16)],
        compiler_params=PARAMS,
        name=f"merge_{level}",
    )(place, mine, theirs, bank)


def body(echoes, transmit_chirp, band_weights, band_offsets, band_widths, child_rows):
    count = lax.axis_size("range")
    right = lax.ppermute(echoes[:, :, :HALO], "range", [(i + 1, i) for i in range(count - 1)])
    left = lax.ppermute(echoes[:, :, BINS - HALO :], "range", [(i, i + 1) for i in range(count - 1)])
    place = jnp.stack(
        [lax.axis_index("aperture"), lax.axis_index("range"), jnp.int32(BINS * count)]
    ).astype(jnp.int32)
    toeplitz, bank = prepare(
        place, transmit_chirp, band_weights, band_offsets, band_widths, child_rows
    )
    kept, sent = compress(place, echoes, left, right, toeplitz)
    blocks = lax.axis_size("aperture")
    for level in range(LEVELS):
        theirs = lax.ppermute(sent, "aperture", [(i, i ^ (1 << level)) for i in range(blocks)])
        result = merge(place, kept, theirs, bank, level)
        if level + 1 < LEVELS:
            kept, sent = result
    return result


def solution(mesh):
    return jax.shard_map(
        body,
        mesh=mesh,
        in_specs=(
            P(None, "aperture", "range"),
            P(),
            P(None, None, None, "aperture", None),
            P(None, None, "aperture"),
            P(None, None, "aperture"),
            P(None, "aperture"),
        ),
        out_specs=P(None, "aperture", "range"),
        check_vma=False,
    )
```

```python
import jax
import jax.numpy as jnp
from jax import lax
from jax.experimental import pallas as pl
from jax.experimental.pallas import tpu as pltpu
from jax.sharding import PartitionSpec as P

KERN = 16
SHIFT = 16
LEVELS = 4
TAPS = 512
HALF = 16
ROWS = 32
LANES = 128
BINS = 1024
RIM = 128
FRAME = BINS + 2 * RIM
RIM_LATE = 64
FRAME_LATE = BINS + 2 * RIM_LATE
HALO = RIM + TAPS // 2
SPAN = LANES + TAPS
COARSE = 6
FINE = 8
COLS = 2 * COARSE * 32
OUTS = FINE * 32
PART = 64
VMEM = 48 * 1024 * 1024
BF16 = jnp.bfloat16
F32 = jnp.float32


def build_bank(bank, weights, numbers):
    lane = lax.broadcasted_iota(jnp.int32, (HALF, LANES), 1)
    imag = ((lane >> 4) & 1) == 1
    swapped = jnp.where(imag, pltpu.roll(weights, 16, 1), pltpu.roll(weights, LANES - 16, 1))
    sources = (jnp.where(imag, -weights, weights), swapped)
    numbers = numbers.astype(jnp.int32)
    column = [jnp.broadcast_to(numbers[:, i : i + 1], (HALF, LANES)) for i in range(5)]
    for tile in range(COLS // LANES):
        spot = lane + tile * LANES
        upper = spot >= COLS // 2
        spot = jnp.where(upper, spot - COLS // 2, spot)
        base = jnp.where(upper, 32, 0) + ((spot >> 4) & 1) * KERN
        first = (spot >> 5) * FINE - SHIFT - jnp.where(upper, column[1], column[0])
        width = jnp.where(upper, column[3], column[2])
        width = jnp.where((spot & 15) == column[4], width, 0)
        at = slice(tile * LANES, (tile + 1) * LANES)
        rest_at = slice(COLS + tile * LANES, COLS + (tile + 1) * LANES)
        for b in range(FINE):
            tap = first + b
            live = (tap >= 0) & (tap < width)
            index = base | (tap & (KERN - 1))
            for part in range(2):
                value = jnp.take_along_axis(
                    sources[part], index, axis=1, mode="promise_in_bounds"
                )
                value = jnp.where(live, value, 0.0)
                high = value.astype(BF16)
                rows = slice(b * 32 + part * HALF, b * 32 + (part + 1) * HALF)
                bank[rows, at] = high
                bank[rows, rest_at] = (value - high.astype(F32)).astype(BF16)


def level_params(weights, numbers, level, rows):
    tile = weights[rows, (level // 2) * LANES : (level // 2 + 1) * LANES]
    if level % 2:
        tile = pltpu.roll(tile, LANES - PART, 1)
    own = numbers[rows, :]
    picks = (2 * level, 2 * level + 1, 8 + 2 * level, 9 + 2 * level, 16 + level)
    return tile, jnp.concatenate([own[:, i : i + 1] for i in picks], axis=1)


def prepare_kernel(
    place, chirp_hbm, weights_hbm, offsets_hbm, widths_hbm, child_hbm,
    toeplitz, bank, weights, numbers,
    chirp, wide, offsets, widths, child, table, sems,
):
    copies = [
        pltpu.make_async_copy(source, target, sems.at[i])
        for i, (source, target) in enumerate(
            (
                (chirp_hbm, chirp),
                (weights_hbm, wide),
                (offsets_hbm, offsets),
                (widths_hbm, widths),
                (child_hbm, child),
            )
        )
    ]
    for copy in copies:
        copy.start()
    for copy in copies:
        copy.wait()

    taps = chirp[...].astype(F32)
    taps = jnp.concatenate([taps, jnp.zeros((2, SPAN - TAPS), F32)], axis=1)
    real = pltpu.roll(jnp.broadcast_to(taps[0:1], (LANES, SPAN)), 0, 1, stride=1, stride_axis=0)
    imag = pltpu.roll(jnp.broadcast_to(taps[1:2], (LANES, SPAN)), 0, 1, stride=1, stride_axis=0)
    toeplitz[0:LANES, 0:SPAN] = real.astype(BF16)
    toeplitz[0:LANES, SPAN : 2 * SPAN] = imag.astype(BF16)
    toeplitz[LANES : 2 * LANES, 0:SPAN] = (-imag).astype(BF16)
    toeplitz[LANES : 2 * LANES, SPAN : 2 * SPAN] = real.astype(BF16)

    weights[...] = wide[...].T
    table[...] = jnp.zeros((ROWS, LANES), F32)
    for level in range(LEVELS):
        table[2 * level : 2 * level + 2, 0:ROWS] = offsets[level].astype(F32)
        table[8 + 2 * level : 10 + 2 * level, 0:ROWS] = widths[level].astype(F32)
    table[16:20, 0:ROWS] = child[...].astype(F32)
    numbers[:, 0:ROWS] = table[...].T[0:ROWS]

    first = pl.multiple_of(((place[0] >> 1) & 1) * HALF, HALF)
    other = pl.multiple_of((1 - ((place[0] >> 1) & 1)) * HALF, HALF)
    for half, start in enumerate((first, other)):
        build_bank(bank.at[half], *level_params(weights, numbers, 0, pl.ds(start, HALF)))


def prepare_late_kernel(after, weights, numbers, bank, bank_last, payload):
    for half in range(2):
        rows = slice(half * HALF, (half + 1) * HALF)
        build_bank(bank.at[half], *level_params(weights, numbers, 1, rows))
        build_bank(bank_last.at[half], *level_params(weights, numbers, 3, rows))
        tile, own = level_params(weights, numbers, 2, rows)
        lane = lax.broadcasted_iota(jnp.int32, (HALF, LANES), 1)
        high = tile.astype(BF16).astype(F32)
        rest = pltpu.roll(tile - high, PART, 1)
        payload[half, 0:HALF] = jnp.where(lane < PART, high, rest).astype(BF16)
        own = jnp.concatenate([own, jnp.zeros((HALF, LANES - 5), F32)], axis=1)
        payload[half, HALF:ROWS] = own.astype(BF16)


def inside_mask(place, rows, length, rim):
    bins = lax.broadcasted_iota(jnp.int32, (rows, length), 1) + (place[1] * BINS - rim)
    return (bins >= 0) & (bins < place[2])


def compress_kernel(place, echoes, left, right, toeplitz, kept, sent, window):
    start = pl.multiple_of((place[0] & 1) * HALF, HALF)
    other = pl.multiple_of((1 - (place[0] & 1)) * HALF, HALF)
    blocks = FRAME // LANES
    tiles = SPAN // LANES
    first = HALO // LANES
    last = first + BINS // LANES
    for part in range(2):
        for half, at in enumerate((start, other)):
            for tile in range(blocks + tiles - 1):
                if tile < first:
                    piece = left[part, pl.ds(at, HALF), tile * LANES : (tile + 1) * LANES]
                elif tile < last:
                    spot = (tile - first) * LANES
                    piece = echoes[part, pl.ds(at, HALF), spot : spot + LANES]
                else:
                    spot = (tile - last) * LANES
                    piece = right[part, pl.ds(at, HALF), spot : spot + LANES]
                for block in range(max(0, tile - tiles + 1), min(blocks, tile + 1)):
                    spot = part * SPAN + (tile - block) * LANES
                    top = block * ROWS + half * HALF
                    window[top : top + HALF, spot : spot + LANES] = piece
    result = lax.dot_general(
        window[...], toeplitz[...], (((1,), (1,)), ((), ())), preferred_element_type=jnp.float32
    )
    position = place[1] * BINS - RIM
    for block in range(blocks):
        bins = lax.broadcasted_iota(jnp.int32, (ROWS, 2 * LANES), 1) & (LANES - 1)
        bins = bins + (position + block * LANES)
        inside = (bins >= 0) & (bins < place[2])
        piece = jnp.where(inside, result[block * ROWS : (block + 1) * ROWS], 0.0)
        piece = piece.astype(jnp.bfloat16)
        at = slice(block * LANES, (block + 1) * LANES)
        for part in range(2):
            lanes = slice(part * LANES, (part + 1) * LANES)
            kept[part * HALF : (part + 1) * HALF, at] = piece[0:HALF, lanes]
            sent[part * HALF : (part + 1) * HALF, at] = piece[HALF:ROWS, lanes]


def fill_stack(stack, t, source):
    length = source.shape[1]
    source = source.astype(F32)
    for a in range(COARSE):
        shift = (24 - 8 * a) % length
        moved = (pltpu.roll(source, shift, 1) if shift else source).astype(BF16)
        top = t * (COLS // 2) + a * 32
        stack[top : top + 32] = moved
        stack[COLS + top : COLS + top + 32] = moved


def fine_sum(product, trim):
    length = product.shape[1]
    total = None
    for b in range(FINE):
        piece = product[b * 32 : (b + 1) * 32]
        if b + trim:
            piece = pltpu.roll(piece, length - b - trim, 1)
        total = piece if total is None else total + piece
    return total


def merge_first_kernel(place, mine, theirs, bank, kept, sent, stack):
    lower = (place[0] & 1) == 0
    fill_stack(stack, 0, jnp.where(lower, mine[...], theirs[...]))
    fill_stack(stack, 1, jnp.where(lower, theirs[...], mine[...]))
    inside = inside_mask(place, 32, FRAME, RIM)
    for half, out in enumerate((kept, sent)):
        product = jnp.dot(bank[half], stack[...], preferred_element_type=F32)
        out[...] = jnp.where(inside, fine_sum(product, 0), 0.0).astype(BF16)


def merge_second_kernel(place, mine, theirs, bank, payload, out, stack):
    lower = ((place[0] >> 1) & 1) == 0
    fill_stack(stack, 0, jnp.where(lower, mine[...], theirs[...]))
    fill_stack(stack, 1, jnp.where(lower, theirs[...], mine[...]))
    inside = inside_mask(place, 32, FRAME_LATE, RIM_LATE)
    for half in range(2):
        product = jnp.dot(bank[half], stack[...], preferred_element_type=F32)
        total = fine_sum(product, RIM - RIM_LATE)[:, 0:FRAME_LATE]
        total = jnp.where(inside, total, 0.0).astype(BF16)
        for q in (half, half + 2):
            out[q, :, 0:FRAME_LATE] = total
            out[q, :, FRAME_LATE:FRAME] = payload[q >> 1]


def merge_late_kernel(place, parts, bank_last, out, bank, stacks):
    inside = inside_mask(place, 32, FRAME_LATE, RIM_LATE)
    side = (place[0] >> 2) & 1
    for beta in range(2):
        packed = parts[2 * beta + side, :, FRAME_LATE:FRAME].astype(F32)
        weights = packed[0:HALF] + pltpu.roll(packed[0:HALF], LANES - PART, 1)
        build_bank(bank.at[beta], weights, packed[HALF:ROWS])
        for t in range(2):
            fill_stack(stacks.at[beta], t, parts[2 * beta + t, :, 0:FRAME_LATE])
    for beta in range(2):
        product = jnp.dot(bank[beta], stacks[beta], preferred_element_type=F32)
        total = jnp.where(inside, fine_sum(product, 0), 0.0).astype(BF16)
        fill_stack(stacks.at[2], beta, total)
    for half in range(2):
        product = jnp.dot(bank_last[half], stacks[2], preferred_element_type=F32)
        total = fine_sum(product, RIM_LATE)[:, 0:BINS].astype(BF16)
        for part in range(2):
            out[part, half * HALF : (half + 1) * HALF] = total[part * HALF : (part + 1) * HALF]


WHOLE = pl.BlockSpec(memory_space=pltpu.VMEM)
SCALARS = pl.BlockSpec(memory_space=pltpu.SMEM)
FAR = pl.BlockSpec(memory_space=pltpu.HBM)
PARAMS = pltpu.CompilerParams(vmem_limit_bytes=VMEM)
BANK = jax.ShapeDtypeStruct((2, OUTS, 2 * COLS), BF16)
MESSAGE = jax.ShapeDtypeStruct((2 * HALF, FRAME), BF16)


def prepare(place, chirp, weights, offsets, widths, child):
    return pl.pallas_call(
        prepare_kernel,
        out_shape=(
            jax.ShapeDtypeStruct((2 * LANES, 2 * SPAN), BF16),
            BANK,
            jax.ShapeDtypeStruct((ROWS, 4 * PART), F32),
            jax.ShapeDtypeStruct((ROWS, LANES), F32),
        ),
        in_specs=[SCALARS] + [FAR] * 5,
        out_specs=(WHOLE,) * 4,
        scratch_shapes=[
            pltpu.VMEM(chirp.shape, chirp.dtype),
            pltpu.VMEM(weights.shape, weights.dtype),
            pltpu.VMEM(offsets.shape, offsets.dtype),
            pltpu.VMEM(widths.shape, widths.dtype),
            pltpu.VMEM(child.shape, child.dtype),
            pltpu.VMEM((ROWS, LANES), F32),
            pltpu.SemaphoreType.DMA((5,)),
        ],
        compiler_params=PARAMS,
        cost_estimate=pl.CostEstimate(flops=1_000_000_000, bytes_accessed=2_000_000, transcendentals=0),
        name="prepare",
    )(place, chirp, weights, offsets, widths, child)


def prepare_late(after, weights, numbers):
    return pl.pallas_call(
        prepare_late_kernel,
        out_shape=(BANK, BANK, jax.ShapeDtypeStruct((2, ROWS, LANES), BF16)),
        in_specs=[pl.BlockSpec(memory_space=pl.ANY), WHOLE, WHOLE],
        out_specs=(WHOLE,) * 3,
        compiler_params=PARAMS,
        cost_estimate=pl.CostEstimate(flops=2_000_000_000, bytes_accessed=4_000_000, transcendentals=0),
        name="prepare_late",
    )(after, weights, numbers)


def compress(place, echoes, left, right, toeplitz):
    return pl.pallas_call(
        compress_kernel,
        out_shape=(MESSAGE, MESSAGE),
        in_specs=[SCALARS] + [WHOLE] * 4,
        out_specs=(WHOLE, WHOLE),
        scratch_shapes=[pltpu.VMEM((FRAME // LANES * ROWS, 2 * SPAN), BF16)],
        compiler_params=PARAMS,
        name="compress",
    )(place, echoes, left, right, toeplitz)


def merge_first(place, mine, theirs, bank):
    return pl.pallas_call(
        merge_first_kernel,
        out_shape=(MESSAGE, MESSAGE),
        in_specs=[SCALARS] + [WHOLE] * 3,
        out_specs=(WHOLE, WHOLE),
        scratch_shapes=[pltpu.VMEM((2 * COLS, FRAME), BF16)],
        compiler_params=PARAMS,
        name="merge_first",
    )(place, mine, theirs, bank)


def merge_second(place, mine, theirs, bank, payload):
    return pl.pallas_call(
        merge_second_kernel,
        out_shape=jax.ShapeDtypeStruct((4, 2 * HALF, FRAME), BF16),
        in_specs=[SCALARS] + [WHOLE] * 4,
        out_specs=WHOLE,
        scratch_shapes=[pltpu.VMEM((2 * COLS, FRAME), BF16)],
        compiler_params=PARAMS,
        name="merge_second",
    )(place, mine, theirs, bank, payload)


def merge_late(place, parts, bank_last):
    return pl.pallas_call(
        merge_late_kernel,
        out_shape=jax.ShapeDtypeStruct((2, ROWS, BINS), BF16),
        in_specs=[SCALARS] + [WHOLE] * 2,
        out_specs=WHOLE,
        scratch_shapes=[
            pltpu.VMEM((2, OUTS, 2 * COLS), BF16),
            pltpu.VMEM((3, 2 * COLS, FRAME_LATE), BF16),
        ],
        compiler_params=PARAMS,
        name="merge_late",
    )(place, parts, bank_last)


def body(echoes, transmit_chirp, band_weights, band_offsets, band_widths, child_rows):
    count = lax.axis_size("range")
    right = lax.ppermute(echoes[:, :, :HALO], "range", [(i + 1, i) for i in range(count - 1)])
    left = lax.ppermute(echoes[:, :, BINS - HALO :], "range", [(i, i + 1) for i in range(count - 1)])
    place = jnp.stack(
        [lax.axis_index("aperture"), lax.axis_index("range"), jnp.int32(BINS * count)]
    ).astype(jnp.int32)
    taps_first = jnp.swapaxes(band_weights, 3, 4).reshape(LEVELS * PART, ROWS)
    toeplitz, bank, weights, numbers = prepare(
        place, transmit_chirp, taps_first, band_offsets, band_widths, child_rows
    )
    kept, sent = compress(place, echoes, left, right, toeplitz)
    blocks = lax.axis_size("aperture")
    theirs = lax.ppermute(sent, "aperture", [(i, i ^ 1) for i in range(blocks)])
    kept, sent = merge_first(place, kept, theirs, bank)
    theirs = lax.ppermute(sent, "aperture", [(i, i ^ 2) for i in range(blocks)])
    bank, bank_last, payload = prepare_late(kept, weights, numbers)
    parts = merge_second(place, kept, theirs, bank, payload)
    groups = [[i, i + 4, i + 8, i + 12] for i in range(blocks) if not i & 12]
    parts = lax.all_to_all(parts, "aperture", 0, 0, axis_index_groups=groups, tiled=True)
    return merge_late(place, parts, bank_last)


def solution(mesh):
    return jax.shard_map(
        body,
        mesh=mesh,
        in_specs=(
            P(None, "aperture", "range"),
            P(),
            P(None, None, None, "aperture", None),
            P(None, None, "aperture"),
            P(None, None, "aperture"),
            P(None, "aperture"),
        ),
        out_specs=P(None, "aperture", "range"),
        check_vma=False,
    )
```

```python
import functools

import jax
import jax.numpy as jnp
from jax import lax
from jax.experimental import pallas as pl
from jax.experimental.pallas import tpu as pltpu
from jax.sharding import PartitionSpec as P

KERN = 16
SHIFT = 16
LEVELS = 4
TAPS = 512
HALF = 16
ROWS = 32
LANES = 128
BINS = 1024
RIM = 128
FRAME = BINS + 2 * RIM
RIM_LATE = 64
FRAME_LATE = BINS + 2 * RIM_LATE
HALO = RIM + TAPS // 2
SPAN = LANES + TAPS
COARSE = 6
FINE = 8
COLS = 2 * COARSE * 32
OUTS = FINE * 32
PART = 64
VMEM = 48 * 1024 * 1024
BF16 = jnp.bfloat16
F32 = jnp.float32


def build_bank(bank, weights, numbers):
    lane = lax.broadcasted_iota(jnp.int32, (HALF, LANES), 1)
    imag = ((lane >> 4) & 1) == 1
    swapped = jnp.where(imag, pltpu.roll(weights, 16, 1), pltpu.roll(weights, LANES - 16, 1))
    sources = (jnp.where(imag, -weights, weights), swapped)
    numbers = numbers.astype(jnp.int32)
    column = [jnp.broadcast_to(numbers[:, i : i + 1], (HALF, LANES)) for i in range(5)]
    for tile in range(COLS // LANES):
        spot = lane + tile * LANES
        upper = spot >= COLS // 2
        spot = jnp.where(upper, spot - COLS // 2, spot)
        base = jnp.where(upper, 32, 0) + ((spot >> 4) & 1) * KERN
        first = (spot >> 5) * FINE - SHIFT - jnp.where(upper, column[1], column[0])
        width = jnp.where(upper, column[3], column[2])
        width = jnp.where((spot & 15) == column[4], width, 0)
        at = slice(tile * LANES, (tile + 1) * LANES)
        rest_at = slice(COLS + tile * LANES, COLS + (tile + 1) * LANES)
        for b in range(FINE):
            tap = first + b
            live = (tap >= 0) & (tap < width)
            index = base | (tap & (KERN - 1))
            for part in range(2):
                value = jnp.take_along_axis(
                    sources[part], index, axis=1, mode="promise_in_bounds"
                )
                value = jnp.where(live, value, 0.0)
                high = value.astype(BF16)
                rows = slice(b * 32 + part * HALF, b * 32 + (part + 1) * HALF)
                bank[rows, at] = high
                bank[rows, rest_at] = (value - high.astype(F32)).astype(BF16)


def level_params(weights, numbers, level, rows):
    swap = ((lax.axis_index("aperture") >> level) & 1) == 1
    tile = weights[rows, (level // 2) * LANES : (level // 2 + 1) * LANES]
    if level % 2:
        tile = pltpu.roll(tile, LANES - PART, 1)
    lane = lax.broadcasted_iota(jnp.int32, (HALF, LANES), 1)
    turned = jnp.where(lane < 32, pltpu.roll(tile, LANES - 32, 1), pltpu.roll(tile, 32, 1))
    own = numbers[rows, :]
    off, wide = 2 * level, 8 + 2 * level
    picks = [own[:, k : k + 1] for k in (off, off + 1, wide, wide + 1, 16 + level)]
    for k in (0, 2):
        pair = picks[k], picks[k + 1]
        picks[k] = jnp.where(swap, pair[1], pair[0])
        picks[k + 1] = jnp.where(swap, pair[0], pair[1])
    return jnp.where(swap, turned, tile), jnp.concatenate(picks, axis=1)


def build_level(bank, weights, numbers, level):
    first = 0
    if level + 1 < LEVELS:
        first = (lax.axis_index("aperture") >> (level + 1)) & 1
    for half in range(2):
        side = half ^ first
        start = side * HALF if isinstance(side, int) else pl.multiple_of(side * HALF, HALF)
        build_bank(bank.at[half], *level_params(weights, numbers, level, pl.ds(start, HALF)))


def prepare_kernel(chirp, taps_in, numbers_in, toeplitz, bank, weights, numbers, table):
    taps = chirp[...].astype(F32)
    taps = jnp.concatenate([taps, jnp.zeros((2, SPAN - TAPS), F32)], axis=1)
    real = pltpu.roll(jnp.broadcast_to(taps[0:1], (LANES, SPAN)), 0, 1, stride=1, stride_axis=0)
    imag = pltpu.roll(jnp.broadcast_to(taps[1:2], (LANES, SPAN)), 0, 1, stride=1, stride_axis=0)
    toeplitz[0:LANES, 0:SPAN] = real.astype(BF16)
    toeplitz[0:LANES, SPAN : 2 * SPAN] = imag.astype(BF16)
    toeplitz[LANES : 2 * LANES, 0:SPAN] = (-imag).astype(BF16)
    toeplitz[LANES : 2 * LANES, SPAN : 2 * SPAN] = real.astype(BF16)

    table[...] = jnp.zeros((ROWS, LANES), F32)
    for level in range(LEVELS):
        weights[:, level * PART : (level + 1) * PART] = taps_in[level].T
        own = numbers_in[level].astype(F32)
        table[2 * level : 2 * level + 2, 0:ROWS] = own[0:2]
        table[8 + 2 * level : 10 + 2 * level, 0:ROWS] = own[2:4]
        table[16 + level : 17 + level, 0:ROWS] = own[4:5]
    numbers[:, 0:ROWS] = table[...].T[0:ROWS]
    build_level(bank, weights, numbers, 0)


def prepare_late_kernel(level, after, weights, numbers, bank):
    build_level(bank, weights, numbers, level)


def inside_mask(rows, length, rim):
    bins = lax.broadcasted_iota(jnp.int32, (rows, length), 1) + (lax.axis_index("range") * BINS - rim)
    return (bins >= 0) & (bins < (BINS * lax.axis_size("range")))


def compress_kernel(sent, echoes, even, odd, toeplitz, out, window, rows=None):
    side = (lax.axis_index("aperture") & 1) ^ 1 if sent else lax.axis_index("aperture") & 1
    at = pl.multiple_of(side * HALF, HALF)
    is_odd = (lax.axis_index("range") & 1) == 1
    blocks = FRAME // LANES
    tiles = SPAN // LANES
    first = HALO // LANES
    last = first + BINS // LANES
    for part in range(2):
        for tile in range(blocks + tiles - 1):
            if first <= tile < last:
                spot = (tile - first) * LANES
                piece = echoes[part, pl.ds(at, HALF), spot : spot + LANES]
            else:
                spot = (tile if tile < first else tile - last) * LANES
                ours = even[part, pl.ds(at, HALF), spot : spot + LANES]
                other = odd[part, pl.ds(at, HALF), spot : spot + LANES]
                if tile < first:
                    piece = jnp.where(is_odd, ours, other)
                else:
                    piece = jnp.where(is_odd, other, ours)
            for block in range(max(0, tile - tiles + 1), min(blocks, tile + 1)):
                spot = part * SPAN + (tile - block) * LANES
                window[block * HALF : (block + 1) * HALF, spot : spot + LANES] = piece
    result = lax.dot_general(
        window[...], toeplitz[...], (((1,), (1,)), ((), ())), preferred_element_type=F32
    )
    position = lax.axis_index("range") * BINS - RIM
    target = out if sent else rows
    for block in range(blocks):
        bins = lax.broadcasted_iota(jnp.int32, (HALF, 2 * LANES), 1) & (LANES - 1)
        bins = bins + (position + block * LANES)
        inside = (bins >= 0) & (bins < BINS * lax.axis_size("range"))
        piece = jnp.where(inside, result[block * HALF : (block + 1) * HALF], 0.0).astype(BF16)
        at = slice(block * LANES, (block + 1) * LANES)
        for part in range(2):
            target[part * HALF : (part + 1) * HALF, at] = piece[:, part * LANES : (part + 1) * LANES]
    if not sent:
        fill_stack(out, rows[...])


def fill_stack(stack, source):
    length = source.shape[1]
    source = source.astype(F32)
    for a in range(COARSE):
        shift = (24 - 8 * a) % length
        moved = pltpu.roll(source, shift, 1) if shift else source
        stack[a * 32 : (a + 1) * 32] = moved.astype(BF16)


def fine_sum(product, trim):
    length = product.shape[1]
    total = None
    for b in range(FINE):
        piece = product[b * 32 : (b + 1) * 32]
        if b + trim:
            piece = pltpu.roll(piece, length - b - trim, 1)
        total = piece if total is None else total + piece
    return total


def product_of(bank, own, partner, trim):
    both = jnp.concatenate([own[...], partner[...]] * 2, axis=0)
    return fine_sum(jnp.dot(bank, both, preferred_element_type=F32), trim)


def rounded(total, rim):
    total = total[:, 0 : BINS + 2 * rim]
    return jnp.where(inside_mask(*total.shape, rim), total, 0.0).astype(BF16)


def merge_sent_kernel(trim, rim, own, theirs, bank, sent, partner):
    fill_stack(partner, theirs[...])
    sent[...] = rounded(product_of(bank[1], own, partner, trim), rim)


def merge_kept_kernel(trim, rim, own, partner, bank, after):
    fill_stack(after, rounded(product_of(bank[0], own, partner, trim), rim))


def merge_last_kernel(own, theirs, bank, out, partner):
    fill_stack(partner, theirs[...])
    for half in range(2):
        total = product_of(bank[half], own, partner, RIM_LATE)[:, 0:BINS].astype(BF16)
        for part in range(2):
            out[part, half * HALF : (half + 1) * HALF] = total[part * HALF : (part + 1) * HALF]


WHOLE = pl.BlockSpec(memory_space=pltpu.VMEM)
PARAMS = pltpu.CompilerParams(vmem_limit_bytes=VMEM)
BANK = jax.ShapeDtypeStruct((2, OUTS, 2 * COLS), BF16)
FRAMES = (FRAME, FRAME, FRAME_LATE, FRAME_LATE)
RIMS = (RIM, RIM, RIM_LATE, RIM_LATE)


def message(length):
    return jax.ShapeDtypeStruct((2 * HALF, length), BF16)


def shifted(length):
    return jax.ShapeDtypeStruct((COLS // 2, length), BF16)


def small_cost():
    return pl.CostEstimate(flops=1000, bytes_accessed=1000, transcendentals=0)


def prepare(chirp, taps, numbers):
    return pl.pallas_call(
        prepare_kernel,
        out_shape=(
            jax.ShapeDtypeStruct((2 * LANES, 2 * SPAN), BF16),
            BANK,
            jax.ShapeDtypeStruct((ROWS, 4 * PART), F32),
            jax.ShapeDtypeStruct((ROWS, LANES), F32),
        ),
        in_specs=[WHOLE] * 3,
        out_specs=(WHOLE,) * 4,
        scratch_shapes=[pltpu.VMEM((ROWS, LANES), F32)],
        compiler_params=PARAMS,
        cost_estimate=pl.CostEstimate(flops=1_000_000_000, bytes_accessed=2_000_000, transcendentals=0),
        name="prepare",
    )(chirp, taps, numbers)


def prepare_late(level, after, weights, numbers):
    return pl.pallas_call(
        functools.partial(prepare_late_kernel, level),
        out_shape=BANK,
        in_specs=[pl.BlockSpec(memory_space=pl.ANY), WHOLE, WHOLE],
        out_specs=WHOLE,
        compiler_params=PARAMS,
        cost_estimate=small_cost(),
        name=f"prepare_{level}",
    )(after, weights, numbers)


def compress(sent, echoes, even, odd, toeplitz):
    scratch = [pltpu.VMEM((FRAME // LANES * HALF, 2 * SPAN), BF16)]
    if not sent:
        scratch.append(pltpu.VMEM((2 * HALF, FRAME), BF16))
    return pl.pallas_call(
        functools.partial(compress_kernel, sent),
        out_shape=message(FRAME) if sent else shifted(FRAME),
        in_specs=[WHOLE] * 4,
        out_specs=WHOLE,
        scratch_shapes=scratch,
        compiler_params=PARAMS,
        cost_estimate=pl.CostEstimate(flops=200_000_000, bytes_accessed=1_000_000, transcendentals=0),
        name="compress_sent" if sent else "compress_kept",
    )(echoes, even, odd, toeplitz)


def merge_sent(level, own, theirs, bank):
    rim = RIMS[level + 1]
    return pl.pallas_call(
        functools.partial(merge_sent_kernel, RIMS[level] - rim, rim),
        out_shape=(message(FRAMES[level + 1]), shifted(FRAMES[level])),
        in_specs=[WHOLE] * 3,
        out_specs=(WHOLE, WHOLE),
        compiler_params=PARAMS,
        name=f"merge_{level}_sent",
    )(own, theirs, bank)


def merge_kept(level, own, partner, bank):
    rim = RIMS[level + 1]
    return pl.pallas_call(
        functools.partial(merge_kept_kernel, RIMS[level] - rim, rim),
        out_shape=shifted(FRAMES[level + 1]),
        in_specs=[WHOLE] * 3,
        out_specs=WHOLE,
        compiler_params=PARAMS,
        cost_estimate=small_cost(),
        name=f"merge_{level}_kept",
    )(own, partner, bank)


def merge_last(own, theirs, bank):
    return pl.pallas_call(
        merge_last_kernel,
        out_shape=jax.ShapeDtypeStruct((2, ROWS, BINS), BF16),
        in_specs=[WHOLE] * 3,
        out_specs=WHOLE,
        scratch_shapes=[pltpu.VMEM((COLS // 2, FRAMES[LEVELS - 1]), BF16)],
        compiler_params=PARAMS,
        name="merge_last",
    )(own, theirs, bank)


def body(echoes, transmit_chirp, band_weights, band_offsets, band_widths, child_rows):
    count = lax.axis_size("range")
    is_odd = lax.axis_index("range") % 2 == 1
    head = echoes[:, :, :HALO]
    tail = echoes[:, :, BINS - HALO :]
    pairs = [(i, i + 1) for i in range(1, count - 1, 2)]
    odd = lax.ppermute(jnp.where(is_odd, tail, head), "range", pairs + [(j, i) for i, j in pairs])
    pairs = [(i, i + 1) for i in range(0, count - 1, 2)]
    even = lax.ppermute(jnp.where(is_odd, head, tail), "range", pairs + [(j, i) for i, j in pairs])
    taps = jnp.swapaxes(band_weights, 3, 4).reshape(LEVELS, PART, ROWS)
    numbers = jnp.concatenate([band_offsets, band_widths, child_rows[:, None]], axis=1)
    toeplitz, bank, weights, numbers = prepare(transmit_chirp, taps, numbers)
    sent = compress(True, echoes, even, odd, toeplitz)
    blocks = lax.axis_size("aperture")
    own = None
    for level in range(LEVELS):
        theirs = lax.ppermute(sent, "aperture", [(i, i ^ (1 << level)) for i in range(blocks)])
        if level == 0:
            own = compress(False, echoes, even, odd, toeplitz)
        else:
            own = merge_kept(level - 1, own, partner, bank)
            bank = prepare_late(level, own, weights, numbers)
        if level + 1 < LEVELS:
            sent, partner = merge_sent(level, own, theirs, bank)
    return merge_last(own, theirs, bank)


def solution(mesh):
    return jax.shard_map(
        body,
        mesh=mesh,
        in_specs=(
            P(None, "aperture", "range"),
            P(),
            P(None, None, None, "aperture", None),
            P(None, None, "aperture"),
            P(None, None, "aperture"),
            P(None, "aperture"),
        ),
        out_specs=P(None, "aperture", "range"),
        check_vma=False,
    )
```

```python
import functools

import jax
import jax.numpy as jnp
from jax import lax
from jax.experimental import pallas as pl
from jax.experimental.pallas import tpu as pltpu
from jax.sharding import PartitionSpec as P

KERN = 16
SHIFT = 16
LEVELS = 4
TAPS = 512
HALF = 16
ROWS = 32
LANES = 128
BINS = 1024
RIM = 128
FRAME = BINS + 2 * RIM
RIM_LATE = 64
FRAME_LATE = BINS + 2 * RIM_LATE
HALO = RIM + TAPS // 2
SPAN = LANES + TAPS
COARSE = 6
FINE = 8
COLS = 2 * COARSE * 32
OUTS = FINE * 32
PART = 64
VMEM = 48 * 1024 * 1024
BF16 = jnp.bfloat16
F32 = jnp.float32


def build_bank(bank, weights, numbers):
    lane = lax.broadcasted_iota(jnp.int32, (HALF, LANES), 1)
    imag = ((lane >> 4) & 1) == 1
    swapped = jnp.where(imag, pltpu.roll(weights, 16, 1), pltpu.roll(weights, LANES - 16, 1))
    sources = (jnp.where(imag, -weights, weights), swapped)
    numbers = numbers.astype(jnp.int32)
    column = [jnp.broadcast_to(numbers[:, i : i + 1], (HALF, LANES)) for i in range(5)]
    for tile in range(COLS // LANES):
        spot = lane + tile * LANES
        upper = spot >= COLS // 2
        spot = jnp.where(upper, spot - COLS // 2, spot)
        base = jnp.where(upper, 32, 0) + ((spot >> 4) & 1) * KERN
        first = (spot >> 5) * FINE - SHIFT - jnp.where(upper, column[1], column[0])
        width = jnp.where(upper, column[3], column[2])
        width = jnp.where((spot & 15) == column[4], width, 0)
        at = slice(tile * LANES, (tile + 1) * LANES)
        rest_at = slice(COLS + tile * LANES, COLS + (tile + 1) * LANES)
        for b in range(FINE):
            tap = first + b
            live = (tap >= 0) & (tap < width)
            index = base | (tap & (KERN - 1))
            for part in range(2):
                value = jnp.take_along_axis(
                    sources[part], index, axis=1, mode="promise_in_bounds"
                )
                value = jnp.where(live, value, 0.0)
                high = value.astype(BF16)
                rows = slice(b * 32 + part * HALF, b * 32 + (part + 1) * HALF)
                bank[rows, at] = high
                bank[rows, rest_at] = (value - high.astype(F32)).astype(BF16)


def level_params(weights, numbers, level, rows):
    swap = ((lax.axis_index("aperture") >> level) & 1) == 1
    tile = weights[rows, (level // 2) * LANES : (level // 2 + 1) * LANES]
    if level % 2:
        tile = pltpu.roll(tile, LANES - PART, 1)
    lane = lax.broadcasted_iota(jnp.int32, (HALF, LANES), 1)
    turned = jnp.where(lane < 32, pltpu.roll(tile, LANES - 32, 1), pltpu.roll(tile, 32, 1))
    own = numbers[rows, :]
    off, wide = 2 * level, 8 + 2 * level
    picks = [own[:, k : k + 1] for k in (off, off + 1, wide, wide + 1, 16 + level)]
    for k in (0, 2):
        pair = picks[k], picks[k + 1]
        picks[k] = jnp.where(swap, pair[1], pair[0])
        picks[k + 1] = jnp.where(swap, pair[0], pair[1])
    return jnp.where(swap, turned, tile), jnp.concatenate(picks, axis=1)


def build_level(bank, weights, numbers, level):
    first = 0
    if level + 1 < LEVELS:
        first = (lax.axis_index("aperture") >> (level + 1)) & 1
    for half in range(2):
        side = half ^ first
        start = side * HALF if isinstance(side, int) else pl.multiple_of(side * HALF, HALF)
        build_bank(bank.at[half], *level_params(weights, numbers, level, pl.ds(start, HALF)))


def prepare_kernel(chirp, taps_in, numbers_in, toeplitz, bank, weights, numbers, table):
    taps = chirp[...].astype(F32)
    taps = jnp.concatenate([taps, jnp.zeros((2, SPAN - TAPS), F32)], axis=1)
    real = pltpu.roll(jnp.broadcast_to(taps[0:1], (LANES, SPAN)), 0, 1, stride=1, stride_axis=0)
    imag = pltpu.roll(jnp.broadcast_to(taps[1:2], (LANES, SPAN)), 0, 1, stride=1, stride_axis=0)
    toeplitz[0:LANES, 0:SPAN] = real.astype(BF16)
    toeplitz[0:LANES, SPAN : 2 * SPAN] = imag.astype(BF16)
    toeplitz[LANES : 2 * LANES, 0:SPAN] = (-imag).astype(BF16)
    toeplitz[LANES : 2 * LANES, SPAN : 2 * SPAN] = real.astype(BF16)

    table[...] = jnp.zeros((ROWS, LANES), F32)
    for level in range(LEVELS):
        weights[:, level * PART : (level + 1) * PART] = taps_in[level].T
        own = numbers_in[level].astype(F32)
        table[2 * level : 2 * level + 2, 0:ROWS] = own[0:2]
        table[8 + 2 * level : 10 + 2 * level, 0:ROWS] = own[2:4]
        table[16 + level : 17 + level, 0:ROWS] = own[4:5]
    numbers[:, 0:ROWS] = table[...].T[0:ROWS]
    build_level(bank, weights, numbers, 0)


def prepare_late_kernel(level, after, weights, numbers, bank):
    build_level(bank, weights, numbers, level)


def inside_mask(rows, length, rim):
    bins = lax.broadcasted_iota(jnp.int32, (rows, length), 1) + (lax.axis_index("range") * BINS - rim)
    return (bins >= 0) & (bins < (BINS * lax.axis_size("range")))


def takes_early(place):
    return place == lax.axis_size("range") // 2


def compress_kernel(sent, echoes, odd, late, early, toeplitz, out, window, rows=None):
    side = (lax.axis_index("aperture") & 1) ^ 1 if sent else lax.axis_index("aperture") & 1
    at = pl.multiple_of(side * HALF, HALF)
    is_odd = (lax.axis_index("range") & 1) == 1
    is_early = takes_early(lax.axis_index("range"))
    blocks = FRAME // LANES
    tiles = SPAN // LANES
    first = HALO // LANES
    last = first + BINS // LANES
    for part in range(2):
        for tile in range(blocks + tiles - 1):
            if first <= tile < last:
                spot = (tile - first) * LANES
                piece = echoes[part, pl.ds(at, HALF), spot : spot + LANES]
            else:
                spot = (tile if tile < first else tile - last) * LANES
                ours = jnp.where(
                    is_early,
                    early[part, pl.ds(at, HALF), spot : spot + LANES],
                    late[part, pl.ds(at, HALF), spot : spot + LANES],
                )
                other = odd[part, pl.ds(at, HALF), spot : spot + LANES]
                if tile < first:
                    piece = jnp.where(is_odd, ours, other)
                else:
                    piece = jnp.where(is_odd, other, ours)
            for block in range(max(0, tile - tiles + 1), min(blocks, tile + 1)):
                spot = part * SPAN + (tile - block) * LANES
                window[block * HALF : (block + 1) * HALF, spot : spot + LANES] = piece
    result = lax.dot_general(
        window[...], toeplitz[...], (((1,), (1,)), ((), ())), preferred_element_type=F32
    )
    position = lax.axis_index("range") * BINS - RIM
    target = out if sent else rows
    for block in range(blocks):
        bins = lax.broadcasted_iota(jnp.int32, (HALF, 2 * LANES), 1) & (LANES - 1)
        bins = bins + (position + block * LANES)
        inside = (bins >= 0) & (bins < BINS * lax.axis_size("range"))
        piece = jnp.where(inside, result[block * HALF : (block + 1) * HALF], 0.0).astype(BF16)
        at = slice(block * LANES, (block + 1) * LANES)
        for part in range(2):
            target[part * HALF : (part + 1) * HALF, at] = piece[:, part * LANES : (part + 1) * LANES]
    if not sent:
        fill_stack(out, rows[...])


def fill_stack(stack, source):
    length = source.shape[1]
    source = source.astype(F32)
    for a in range(COARSE):
        shift = (24 - 8 * a) % length
        moved = pltpu.roll(source, shift, 1) if shift else source
        stack[a * 32 : (a + 1) * 32] = moved.astype(BF16)


def fine_sum(product, trim):
    length = product.shape[1]
    total = None
    for b in range(FINE):
        piece = product[b * 32 : (b + 1) * 32]
        if b + trim:
            piece = pltpu.roll(piece, length - b - trim, 1)
        total = piece if total is None else total + piece
    return total


def product_of(bank, own, partner, trim):
    both = jnp.concatenate([own[...], partner[...]] * 2, axis=0)
    return fine_sum(jnp.dot(bank, both, preferred_element_type=F32), trim)


def rounded(total, rim):
    total = total[:, 0 : BINS + 2 * rim]
    return jnp.where(inside_mask(*total.shape, rim), total, 0.0).astype(BF16)


def merge_sent_kernel(trim, rim, own, theirs, bank, sent, partner):
    fill_stack(partner, theirs[...])
    sent[...] = rounded(product_of(bank[1], own, partner, trim), rim)


def merge_kept_kernel(trim, rim, own, partner, bank, after):
    fill_stack(after, rounded(product_of(bank[0], own, partner, trim), rim))


def merge_last_kernel(own, theirs, bank, out, partner):
    fill_stack(partner, theirs[...])
    for half in range(2):
        total = product_of(bank[half], own, partner, RIM_LATE)[:, 0:BINS].astype(BF16)
        for part in range(2):
            out[part, half * HALF : (half + 1) * HALF] = total[part * HALF : (part + 1) * HALF]


WHOLE = pl.BlockSpec(memory_space=pltpu.VMEM)
PARAMS = pltpu.CompilerParams(vmem_limit_bytes=VMEM)
BANK = jax.ShapeDtypeStruct((2, OUTS, 2 * COLS), BF16)
FRAMES = (FRAME, FRAME, FRAME_LATE, FRAME_LATE)
RIMS = (RIM, RIM, RIM_LATE, RIM_LATE)


def message(length):
    return jax.ShapeDtypeStruct((2 * HALF, length), BF16)


def shifted(length):
    return jax.ShapeDtypeStruct((COLS // 2, length), BF16)


def small_cost():
    return pl.CostEstimate(flops=1000, bytes_accessed=1000, transcendentals=0)


def prepare(chirp, taps, numbers):
    return pl.pallas_call(
        prepare_kernel,
        out_shape=(
            jax.ShapeDtypeStruct((2 * LANES, 2 * SPAN), BF16),
            BANK,
            jax.ShapeDtypeStruct((ROWS, 4 * PART), F32),
            jax.ShapeDtypeStruct((ROWS, LANES), F32),
        ),
        in_specs=[WHOLE] * 3,
        out_specs=(WHOLE,) * 4,
        scratch_shapes=[pltpu.VMEM((ROWS, LANES), F32)],
        compiler_params=PARAMS,
        cost_estimate=pl.CostEstimate(flops=1_000_000_000, bytes_accessed=2_000_000, transcendentals=0),
        name="prepare",
    )(chirp, taps, numbers)


def prepare_late(level, after, weights, numbers):
    return pl.pallas_call(
        functools.partial(prepare_late_kernel, level),
        out_shape=BANK,
        in_specs=[pl.BlockSpec(memory_space=pl.ANY), WHOLE, WHOLE],
        out_specs=WHOLE,
        compiler_params=PARAMS,
        cost_estimate=small_cost(),
        name=f"prepare_{level}",
    )(after, weights, numbers)


def compress(sent, echoes, odd, late, early, toeplitz):
    scratch = [pltpu.VMEM((FRAME // LANES * HALF, 2 * SPAN), BF16)]
    if not sent:
        scratch.append(pltpu.VMEM((2 * HALF, FRAME), BF16))
    return pl.pallas_call(
        functools.partial(compress_kernel, sent),
        out_shape=message(FRAME) if sent else shifted(FRAME),
        in_specs=[WHOLE] * 5,
        out_specs=WHOLE,
        scratch_shapes=scratch,
        compiler_params=PARAMS,
        cost_estimate=pl.CostEstimate(flops=200_000_000, bytes_accessed=1_000_000, transcendentals=0),
        name="compress_sent" if sent else "compress_kept",
    )(echoes, odd, late, early, toeplitz)


def merge_sent(level, own, theirs, bank):
    rim = RIMS[level + 1]
    return pl.pallas_call(
        functools.partial(merge_sent_kernel, RIMS[level] - rim, rim),
        out_shape=(message(FRAMES[level + 1]), shifted(FRAMES[level])),
        in_specs=[WHOLE] * 3,
        out_specs=(WHOLE, WHOLE),
        compiler_params=PARAMS,
        name=f"merge_{level}_sent",
    )(own, theirs, bank)


def merge_kept(level, own, partner, bank):
    rim = RIMS[level + 1]
    return pl.pallas_call(
        functools.partial(merge_kept_kernel, RIMS[level] - rim, rim),
        out_shape=shifted(FRAMES[level + 1]),
        in_specs=[WHOLE] * 3,
        out_specs=WHOLE,
        compiler_params=PARAMS,
        cost_estimate=small_cost(),
        name=f"merge_{level}_kept",
    )(own, partner, bank)


def merge_last(own, theirs, bank):
    return pl.pallas_call(
        merge_last_kernel,
        out_shape=jax.ShapeDtypeStruct((2, ROWS, BINS), BF16),
        in_specs=[WHOLE] * 3,
        out_specs=WHOLE,
        scratch_shapes=[pltpu.VMEM((COLS // 2, FRAMES[LEVELS - 1]), BF16)],
        compiler_params=PARAMS,
        name="merge_last",
    )(own, theirs, bank)


def body(echoes, transmit_chirp, band_weights, band_offsets, band_widths, child_rows):
    count = lax.axis_size("range")
    is_odd = lax.axis_index("range") % 2 == 1
    head = echoes[:, :, :HALO]
    tail = echoes[:, :, BINS - HALO :]
    between = jnp.where(lax.axis_index("range") % 2 == 0, head, tail)
    within = jnp.where(is_odd, head, tail)
    within_late = jnp.where(lax.axis_index("range") % 2 != 1, tail, head)
    pairs = [(i, i + 1) for i in range(1, count - 1, 2)]
    early = lax.ppermute(within, "range", [(i ^ 1, i) for i in range(count) if takes_early(i)])
    odd = lax.ppermute(between, "range", pairs + [(j, i) for i, j in pairs])
    late = lax.ppermute(within_late, "range", [(i ^ 1, i) for i in range(count) if not takes_early(i)])
    taps = jnp.swapaxes(band_weights, 3, 4).reshape(LEVELS, PART, ROWS)
    numbers = jnp.concatenate([band_offsets, band_widths, child_rows[:, None]], axis=1)
    toeplitz, bank, weights, numbers = prepare(transmit_chirp, taps, numbers)
    sent = compress(True, echoes, odd, late, early, toeplitz)
    blocks = lax.axis_size("aperture")
    own = None
    for level in range(LEVELS):
        theirs = lax.ppermute(sent, "aperture", [(i, i ^ (1 << level)) for i in range(blocks)])
        if level == 0:
            own = compress(False, echoes, odd, late, early, toeplitz)
        else:
            own = merge_kept(level - 1, own, partner, bank)
            bank = prepare_late(level, own, weights, numbers)
        if level + 1 < LEVELS:
            sent, partner = merge_sent(level, own, theirs, bank)
    return merge_last(own, theirs, bank)


def solution(mesh):
    return jax.shard_map(
        body,
        mesh=mesh,
        in_specs=(
            P(None, "aperture", "range"),
            P(),
            P(None, None, None, "aperture", None),
            P(None, None, "aperture"),
            P(None, None, "aperture"),
            P(None, "aperture"),
        ),
        out_specs=P(None, "aperture", "range"),
        check_vma=False,
    )
```

```python
import functools

import jax
import jax.numpy as jnp
from jax import lax
from jax.experimental import pallas as pl
from jax.experimental.pallas import tpu as pltpu
from jax.sharding import PartitionSpec as P

KERN = 16
SHIFT = 16
LEVELS = 4
TAPS = 512
HALF = 16
ROWS = 32
LANES = 128
BINS = 1024
RIM = 128
FRAME = BINS + 2 * RIM
RIM_LATE = 64
FRAME_LATE = BINS + 2 * RIM_LATE
HALO = RIM + TAPS // 2
SPAN = LANES + TAPS
COARSE = 6
FINE = 8
COLS = 2 * COARSE * 32
OUTS = FINE * 32
PART = 64
VMEM = 48 * 1024 * 1024
BF16 = jnp.bfloat16
F32 = jnp.float32


def build_bank(bank, weights, numbers):
    lane = lax.broadcasted_iota(jnp.int32, (HALF, LANES), 1)
    imag = ((lane >> 4) & 1) == 1
    swapped = jnp.where(imag, pltpu.roll(weights, 16, 1), pltpu.roll(weights, LANES - 16, 1))
    sources = (jnp.where(imag, -weights, weights), swapped)
    column = [jnp.broadcast_to(number, (HALF, LANES)).astype(jnp.int32) for number in numbers]
    for t in range(2):
        width = jnp.where((lane & 15) == column[4], column[2 + t], 0)
        base = t * 32 + ((lane >> 4) & 1) * KERN
        for tile in range(2):
            coarse = (lane >> 5) if tile == 0 else 4 + ((lane >> 5) & 1)
            first = coarse * FINE - SHIFT - column[t]
            for b in range(FINE):
                tap = first + b
                live = (tap >= 0) & (tap < width)
                index = base | (tap & (KERN - 1))
                for part in range(2):
                    value = jnp.take_along_axis(
                        sources[part], index, axis=1, mode="promise_in_bounds"
                    )
                    value = jnp.where(live, value, 0.0)
                    high = value.astype(BF16).astype(F32)
                    rows = slice(b * 32 + part * HALF, b * 32 + (part + 1) * HALF)
                    at = t * COLS + tile * LANES
                    if tile == 0:
                        bank[rows, at : at + LANES] = high.astype(BF16)
                        bank[rows, at + 2 * LANES : at + 3 * LANES] = (value - high).astype(BF16)
                    else:
                        both = jnp.where(lane < LANES // 2, high, value - high)
                        bank[rows, at : at + LANES] = both.astype(BF16)


def child_rows_of(stack):
    return [stack[0:LANES], stack[LANES:], stack[LANES:], stack[0:LANES]]


def child_product(bank, t, stack):
    rows = jnp.concatenate(child_rows_of(stack), axis=0)
    return jnp.dot(bank[:, t * COLS : (t + 1) * COLS], rows, preferred_element_type=F32)


def both_products(bank, own, partner):
    rows = jnp.concatenate(child_rows_of(own) + child_rows_of(partner), axis=0)
    return jnp.dot(bank[...], rows, preferred_element_type=F32)


def level_params(weights, numbers, level, rows):
    swap = ((lax.axis_index("aperture") >> level) & 1) == 1
    tile = weights[rows, (level // 2) * LANES : (level // 2 + 1) * LANES]
    if level % 2:
        tile = pltpu.roll(tile, LANES - PART, 1)
    lane = lax.broadcasted_iota(jnp.int32, (HALF, LANES), 1)
    turned = jnp.where(lane < 32, pltpu.roll(tile, LANES - 32, 1), pltpu.roll(tile, 32, 1))
    own = numbers[rows, :]
    off, wide = 2 * level, 8 + 2 * level
    picks = [own[:, k : k + 1] for k in (off, off + 1, wide, wide + 1, 16 + level)]
    for k in (0, 2):
        pair = picks[k], picks[k + 1]
        picks[k] = jnp.where(swap, pair[1], pair[0])
        picks[k + 1] = jnp.where(swap, pair[0], pair[1])
    return jnp.where(swap, turned, tile), picks


def build_level(bank, weights, numbers, level):
    first = 0
    if level + 1 < LEVELS:
        first = (lax.axis_index("aperture") >> (level + 1)) & 1
    for half in range(2):
        side = half ^ first
        start = side * HALF if isinstance(side, int) else pl.multiple_of(side * HALF, HALF)
        build_bank(bank.at[half * OUTS : (half + 1) * OUTS], *level_params(weights, numbers, level, pl.ds(start, HALF)))


def prepare_kernel(
    chirp, taps_in, numbers_in, toeplitz, bank, bank_last, weights, numbers, table
):
    taps = chirp[...].astype(F32)
    taps = jnp.concatenate([taps, jnp.zeros((2, SPAN - TAPS), F32)], axis=1)
    real = pltpu.roll(jnp.broadcast_to(taps[0:1], (LANES, SPAN)), 0, 1, stride=1, stride_axis=0)
    imag = pltpu.roll(jnp.broadcast_to(taps[1:2], (LANES, SPAN)), 0, 1, stride=1, stride_axis=0)
    toeplitz[0:LANES, 0:SPAN] = real.astype(BF16)
    toeplitz[0:LANES, SPAN : 2 * SPAN] = imag.astype(BF16)
    toeplitz[LANES : 2 * LANES, 0:SPAN] = (-imag).astype(BF16)
    toeplitz[LANES : 2 * LANES, SPAN : 2 * SPAN] = real.astype(BF16)

    table[...] = jnp.zeros((ROWS, LANES), F32)
    for level in range(LEVELS):
        weights[:, level * PART : (level + 1) * PART] = taps_in[level].T
        own = numbers_in[level].astype(F32)
        table[2 * level : 2 * level + 2, 0:ROWS] = own[0:2]
        table[8 + 2 * level : 10 + 2 * level, 0:ROWS] = own[2:4]
        table[16 + level : 17 + level, 0:ROWS] = own[4:5]
    numbers[:, 0:ROWS] = table[...].T[0:ROWS]
    build_level(bank, weights, numbers, 0)
    build_level(bank_last, weights, numbers, LEVELS - 1)


def banks_kernel(levels, after, weights, numbers, *banks):
    for level, bank in zip(levels, banks):
        build_level(bank, weights, numbers, level)


def bank_and_part_kernel(level, trim, own, weights, numbers, bank, part):
    build_level(bank, weights, numbers, level)
    part[...] = fine_sum(child_product(bank.at[OUTS : 2 * OUTS], 0, own), trim)


def parts_kernel(trim, own, bank, parts):
    product = child_product(bank, 0, own)
    for half in range(2):
        parts[half] = fine_sum(product[half * OUTS : (half + 1) * OUTS], trim)


def inside_mask(rows, length, rim):
    bins = lax.broadcasted_iota(jnp.int32, (rows, length), 1) + (lax.axis_index("range") * BINS - rim)
    return (bins >= 0) & (bins < (BINS * lax.axis_size("range")))


def takes_early(place):
    return place == lax.axis_size("range") // 2


def compress_kernel(sent, echoes, odd, late, early, toeplitz, out, window, rows=None):
    side = (lax.axis_index("aperture") & 1) ^ 1 if sent else lax.axis_index("aperture") & 1
    at = pl.multiple_of(side * HALF, HALF)
    is_odd = (lax.axis_index("range") & 1) == 1
    is_early = takes_early(lax.axis_index("range"))
    blocks = FRAME // LANES
    tiles = SPAN // LANES
    first = HALO // LANES
    last = first + BINS // LANES
    for part in range(2):
        for tile in range(blocks + tiles - 1):
            if first <= tile < last:
                spot = (tile - first) * LANES
                piece = echoes[part, pl.ds(at, HALF), spot : spot + LANES]
            else:
                spot = (tile if tile < first else tile - last) * LANES
                ours = jnp.where(
                    is_early,
                    early[part, pl.ds(at, HALF), spot : spot + LANES],
                    late[part, pl.ds(at, HALF), spot : spot + LANES],
                )
                other = odd[part, pl.ds(at, HALF), spot : spot + LANES]
                if tile < first:
                    piece = jnp.where(is_odd, ours, other)
                else:
                    piece = jnp.where(is_odd, other, ours)
            for block in range(max(0, tile - tiles + 1), min(blocks, tile + 1)):
                spot = part * SPAN + (tile - block) * LANES
                window[block * HALF : (block + 1) * HALF, spot : spot + LANES] = piece
    result = lax.dot_general(
        window[...], toeplitz[...], (((1,), (1,)), ((), ())), preferred_element_type=F32
    )
    position = lax.axis_index("range") * BINS - RIM
    target = out if sent else rows
    for block in range(blocks):
        bins = lax.broadcasted_iota(jnp.int32, (HALF, 2 * LANES), 1) & (LANES - 1)
        bins = bins + (position + block * LANES)
        inside = (bins >= 0) & (bins < BINS * lax.axis_size("range"))
        piece = jnp.where(inside, result[block * HALF : (block + 1) * HALF], 0.0).astype(BF16)
        at = slice(block * LANES, (block + 1) * LANES)
        for part in range(2):
            target[part * HALF : (part + 1) * HALF, at] = piece[:, part * LANES : (part + 1) * LANES]
    if not sent:
        fill_stack(out, rows[...])


def fill_stack(stack, source):
    length = source.shape[1]
    source = source.astype(F32)
    for a in range(COARSE):
        shift = (24 - 8 * a) % length
        moved = pltpu.roll(source, shift, 1) if shift else source
        stack[a * 32 : (a + 1) * 32] = moved.astype(BF16)


def fine_sum(product, trim):
    length = product.shape[1]
    total = None
    for b in range(FINE):
        piece = product[b * 32 : (b + 1) * 32]
        if b + trim:
            piece = pltpu.roll(piece, length - b - trim, 1)
        total = piece if total is None else total + piece
    return total


def rounded(total, rim):
    total = total[:, 0 : BINS + 2 * rim]
    return jnp.where(inside_mask(*total.shape, rim), total, 0.0).astype(BF16)


def merge_sent_kernel(trim, rim, own, theirs, bank, sent, partner):
    fill_stack(partner, theirs[...])
    product = both_products(bank.at[OUTS : 2 * OUTS], own, partner)
    sent[...] = rounded(fine_sum(product, trim), rim)


def merge_sent_part_kernel(trim, rim, part, theirs, bank, sent, partner):
    fill_stack(partner, theirs[...])
    product = child_product(bank.at[OUTS : 2 * OUTS], 1, partner)
    sent[...] = rounded(part[...] + fine_sum(product, trim), rim)


def merge_kept_kernel(trim, rim, own, partner, bank, after):
    product = both_products(bank.at[0:OUTS], own, partner)
    fill_stack(after, rounded(fine_sum(product, trim), rim))


def merge_last_kernel(parts, theirs, bank, out, partner):
    fill_stack(partner, theirs[...])
    product = child_product(bank, 1, partner)
    for half in range(2):
        total = parts[half] + fine_sum(product[half * OUTS : (half + 1) * OUTS], RIM_LATE)
        total = total[:, 0:BINS].astype(BF16)
        for part in range(2):
            out[part, half * HALF : (half + 1) * HALF] = total[part * HALF : (part + 1) * HALF]


WHOLE = pl.BlockSpec(memory_space=pltpu.VMEM)
PARAMS = pltpu.CompilerParams(vmem_limit_bytes=VMEM)
BANK = jax.ShapeDtypeStruct((2 * OUTS, 2 * COLS), BF16)
FRAMES = (FRAME, FRAME, FRAME_LATE, FRAME_LATE)
RIMS = (RIM, RIM, RIM_LATE, RIM_LATE)


def message(length):
    return jax.ShapeDtypeStruct((2 * HALF, length), BF16)


def shifted(length):
    return jax.ShapeDtypeStruct((COLS // 2, length), BF16)


def small_cost():
    return pl.CostEstimate(flops=1000, bytes_accessed=1000, transcendentals=0)


def prepare(chirp, taps, numbers):
    return pl.pallas_call(
        prepare_kernel,
        out_shape=(
            jax.ShapeDtypeStruct((2 * LANES, 2 * SPAN), BF16),
            BANK,
            BANK,
            jax.ShapeDtypeStruct((ROWS, 4 * PART), F32),
            jax.ShapeDtypeStruct((ROWS, LANES), F32),
        ),
        in_specs=[WHOLE] * 3,
        out_specs=(WHOLE,) * 5,
        scratch_shapes=[pltpu.VMEM((ROWS, LANES), F32)],
        compiler_params=PARAMS,
        cost_estimate=pl.CostEstimate(flops=1_000_000_000, bytes_accessed=2_000_000, transcendentals=0),
        name="prepare",
    )(chirp, taps, numbers)


def make_banks(levels, after, weights, numbers):
    return pl.pallas_call(
        functools.partial(banks_kernel, levels),
        out_shape=(BANK,) * len(levels),
        in_specs=[pl.BlockSpec(memory_space=pl.ANY), WHOLE, WHOLE],
        out_specs=(WHOLE,) * len(levels),
        compiler_params=PARAMS,
        cost_estimate=small_cost(),
        name="bank_" + "_".join(map(str, levels)),
    )(after, weights, numbers)


def bank_and_part(level, own, weights, numbers):
    return pl.pallas_call(
        functools.partial(bank_and_part_kernel, level, trim_of(level)),
        out_shape=(BANK, jax.ShapeDtypeStruct((2 * HALF, FRAMES[level]), F32)),
        in_specs=[WHOLE] * 3,
        out_specs=(WHOLE, WHOLE),
        compiler_params=PARAMS,
        cost_estimate=small_cost(),
        name=f"bank_and_part_{level}",
    )(own, weights, numbers)


def own_parts(level, own, bank):
    return pl.pallas_call(
        functools.partial(parts_kernel, trim_of(level)),
        out_shape=jax.ShapeDtypeStruct((2, 2 * HALF, FRAMES[level]), F32),
        in_specs=[WHOLE] * 2,
        out_specs=WHOLE,
        compiler_params=PARAMS,
        cost_estimate=small_cost(),
        name=f"own_parts_{level}",
    )(own, bank)


def trim_of(level):
    return RIMS[level] - RIMS[level + 1] if level + 1 < LEVELS else RIMS[level]


def compress(sent, echoes, odd, late, early, toeplitz):
    scratch = [pltpu.VMEM((FRAME // LANES * HALF, 2 * SPAN), BF16)]
    if not sent:
        scratch.append(pltpu.VMEM((2 * HALF, FRAME), BF16))
    return pl.pallas_call(
        functools.partial(compress_kernel, sent),
        out_shape=message(FRAME) if sent else shifted(FRAME),
        in_specs=[WHOLE] * 5,
        out_specs=WHOLE,
        scratch_shapes=scratch,
        compiler_params=PARAMS,
        cost_estimate=pl.CostEstimate(flops=200_000_000, bytes_accessed=1_000_000, transcendentals=0),
        name="compress_sent" if sent else "compress_kept",
    )(echoes, odd, late, early, toeplitz)


def merge_sent(level, own, theirs, bank, has_part=False):
    kernel = merge_sent_part_kernel if has_part else merge_sent_kernel
    return pl.pallas_call(
        functools.partial(kernel, trim_of(level), RIMS[level + 1]),
        out_shape=(message(FRAMES[level + 1]), shifted(FRAMES[level])),
        in_specs=[WHOLE] * 3,
        out_specs=(WHOLE, WHOLE),
        compiler_params=PARAMS,
        name=f"merge_{level}_sent",
    )(own, theirs, bank)


def merge_kept(level, own, partner, bank):
    return pl.pallas_call(
        functools.partial(merge_kept_kernel, trim_of(level), RIMS[level + 1]),
        out_shape=shifted(FRAMES[level + 1]),
        in_specs=[WHOLE] * 3,
        out_specs=WHOLE,
        compiler_params=PARAMS,
        cost_estimate=small_cost(),
        name=f"merge_{level}_kept",
    )(own, partner, bank)


def merge_last(parts, theirs, bank):
    return pl.pallas_call(
        merge_last_kernel,
        out_shape=jax.ShapeDtypeStruct((2, ROWS, BINS), BF16),
        in_specs=[WHOLE] * 3,
        out_specs=WHOLE,
        scratch_shapes=[pltpu.VMEM((COLS // 2, FRAMES[LEVELS - 1]), BF16)],
        compiler_params=PARAMS,
        name="merge_last",
    )(parts, theirs, bank)


def body(echoes, transmit_chirp, band_weights, band_offsets, band_widths, child_rows):
    count = lax.axis_size("range")
    is_odd = lax.axis_index("range") % 2 == 1
    head = echoes[:, :, :HALO]
    tail = echoes[:, :, BINS - HALO :]
    between = jnp.where(lax.axis_index("range") % 2 == 0, head, tail)
    within = jnp.where(is_odd, head, tail)
    within_late = jnp.where(lax.axis_index("range") % 2 != 1, tail, head)
    pairs = [(i, i + 1) for i in range(1, count - 1, 2)]
    early = lax.ppermute(within, "range", [(i ^ 1, i) for i in range(count) if takes_early(i)])
    odd = lax.ppermute(between, "range", pairs + [(j, i) for i, j in pairs])
    late = lax.ppermute(within_late, "range", [(i ^ 1, i) for i in range(count) if not takes_early(i)])
    taps = jnp.swapaxes(band_weights, 3, 4).reshape(LEVELS, PART, ROWS)
    numbers = jnp.concatenate([band_offsets, band_widths, child_rows[:, None]], axis=1)
    toeplitz, bank, bank_last, weights, numbers = prepare(transmit_chirp, taps, numbers)
    sent = compress(True, echoes, odd, late, early, toeplitz)
    blocks = lax.axis_size("aperture")

    def trade(message, level):
        return lax.ppermute(message, "aperture", [(i, i ^ (1 << level)) for i in range(blocks)])

    theirs = trade(sent, 0)
    own = compress(False, echoes, odd, late, early, toeplitz)
    sent, partner = merge_sent(0, own, theirs, bank)
    theirs = trade(sent, 1)
    own = merge_kept(0, own, partner, bank)
    (bank,) = make_banks((1,), own, weights, numbers)
    sent, partner = merge_sent(1, own, theirs, bank)
    theirs = trade(sent, 2)
    own = merge_kept(1, own, partner, bank)
    bank, part = bank_and_part(2, own, weights, numbers)
    sent, partner = merge_sent(2, part, theirs, bank, True)
    theirs = trade(sent, 3)
    own = merge_kept(2, own, partner, bank)
    parts = own_parts(3, own, bank_last)
    return merge_last(parts, theirs, bank_last)


def solution(mesh):
    return jax.shard_map(
        body,
        mesh=mesh,
        in_specs=(
            P(None, "aperture", "range"),
            P(),
            P(None, None, None, "aperture", None),
            P(None, None, "aperture"),
            P(None, None, "aperture"),
            P(None, "aperture"),
        ),
        out_specs=P(None, "aperture", "range"),
        check_vma=False,
    )
```

```python
import functools

import jax
import jax.numpy as jnp
from jax import lax
from jax.experimental import pallas as pl
from jax.experimental.pallas import tpu as pltpu
from jax.sharding import PartitionSpec as P

KERN = 16
SHIFT = 16
LEVELS = 4
TAPS = 512
HALF = 16
ROWS = 32
LANES = 128
BINS = 1024
RIM = 128
FRAME = BINS + 2 * RIM
RIM_LATE = 64
FRAME_LATE = BINS + 2 * RIM_LATE
HALO = RIM + TAPS // 2
SPAN = LANES + TAPS
COARSE = 6
FINE = 8
COLS = 2 * COARSE * 32
OUTS = FINE * 32
PART = 64
VMEM = 48 * 1024 * 1024
BF16 = jnp.bfloat16
F32 = jnp.float32


def build_bank(bank, weights, numbers):
    lane = lax.broadcasted_iota(jnp.int32, (HALF, LANES), 1)
    imag = ((lane >> 4) & 1) == 1
    swapped = jnp.where(imag, pltpu.roll(weights, 16, 1), pltpu.roll(weights, LANES - 16, 1))
    sources = (jnp.where(imag, -weights, weights), swapped)
    column = [jnp.broadcast_to(number, (HALF, LANES)).astype(jnp.int32) for number in numbers]
    for t in range(2):
        width = jnp.where((lane & 15) == column[4], column[2 + t], 0)
        base = t * 32 + ((lane >> 4) & 1) * KERN
        for tile in range(2):
            coarse = (lane >> 5) if tile == 0 else 4 + ((lane >> 5) & 1)
            first = coarse * FINE - SHIFT - column[t]
            for b in range(FINE):
                tap = first + b
                live = (tap >= 0) & (tap < width)
                index = base | (tap & (KERN - 1))
                for part in range(2):
                    value = jnp.take_along_axis(
                        sources[part], index, axis=1, mode="promise_in_bounds"
                    )
                    value = jnp.where(live, value, 0.0)
                    high = value.astype(BF16).astype(F32)
                    rows = slice(b * 32 + part * HALF, b * 32 + (part + 1) * HALF)
                    at = t * COLS + tile * LANES
                    if tile == 0:
                        bank[rows, at : at + LANES] = high.astype(BF16)
                        bank[rows, at + 2 * LANES : at + 3 * LANES] = (value - high).astype(BF16)
                    else:
                        both = jnp.where(lane < LANES // 2, high, value - high)
                        bank[rows, at : at + LANES] = both.astype(BF16)


def child_rows_of(stack):
    return [stack[0:LANES], stack[LANES:], stack[LANES:], stack[0:LANES]]


def child_product(bank, t, stack):
    rows = jnp.concatenate(child_rows_of(stack), axis=0)
    return jnp.dot(bank[:, t * COLS : (t + 1) * COLS], rows, preferred_element_type=F32)


def both_products(bank, own, partner):
    rows = jnp.concatenate(child_rows_of(own) + child_rows_of(partner), axis=0)
    return jnp.dot(bank[...], rows, preferred_element_type=F32)


def level_params(weights, numbers, level, rows):
    swap = ((lax.axis_index("aperture") >> level) & 1) == 1
    tile = weights[rows, (level // 2) * LANES : (level // 2 + 1) * LANES]
    if level % 2:
        tile = pltpu.roll(tile, LANES - PART, 1)
    lane = lax.broadcasted_iota(jnp.int32, (HALF, LANES), 1)
    turned = jnp.where(lane < 32, pltpu.roll(tile, LANES - 32, 1), pltpu.roll(tile, 32, 1))
    own = numbers[rows, :]
    off, wide = 2 * level, 8 + 2 * level
    picks = [own[:, k : k + 1] for k in (off, off + 1, wide, wide + 1, 16 + level)]
    for k in (0, 2):
        pair = picks[k], picks[k + 1]
        picks[k] = jnp.where(swap, pair[1], pair[0])
        picks[k + 1] = jnp.where(swap, pair[0], pair[1])
    return jnp.where(swap, turned, tile), picks


def build_level(bank, weights, numbers, level):
    first = 0
    if level + 1 < LEVELS:
        first = (lax.axis_index("aperture") >> (level + 1)) & 1
    for half in range(2):
        side = half ^ first
        start = side * HALF if isinstance(side, int) else pl.multiple_of(side * HALF, HALF)
        build_bank(bank.at[half * OUTS : (half + 1) * OUTS], *level_params(weights, numbers, level, pl.ds(start, HALF)))


def prepare_kernel(
    chirp, taps_in, numbers_in, toeplitz, bank, bank_last, weights, numbers, table
):
    taps = chirp[...].astype(F32)
    taps = jnp.concatenate([taps, jnp.zeros((2, SPAN - TAPS), F32)], axis=1)
    real = pltpu.roll(jnp.broadcast_to(taps[0:1], (LANES, SPAN)), 0, 1, stride=1, stride_axis=0)
    imag = pltpu.roll(jnp.broadcast_to(taps[1:2], (LANES, SPAN)), 0, 1, stride=1, stride_axis=0)
    toeplitz[0:LANES, 0:SPAN] = real.astype(BF16)
    toeplitz[0:LANES, SPAN : 2 * SPAN] = imag.astype(BF16)
    toeplitz[LANES : 2 * LANES, 0:SPAN] = (-imag).astype(BF16)
    toeplitz[LANES : 2 * LANES, SPAN : 2 * SPAN] = real.astype(BF16)

    table[...] = jnp.zeros((ROWS, LANES), F32)
    for level in range(LEVELS):
        weights[:, level * PART : (level + 1) * PART] = taps_in[level].T
        own = numbers_in[level].astype(F32)
        table[2 * level : 2 * level + 2, 0:ROWS] = own[0:2]
        table[8 + 2 * level : 10 + 2 * level, 0:ROWS] = own[2:4]
        table[16 + level : 17 + level, 0:ROWS] = own[4:5]
    numbers[:, 0:ROWS] = table[...].T[0:ROWS]
    build_level(bank, weights, numbers, 0)
    build_bank(bank_last, *level_params(weights, numbers, LEVELS - 1, slice(0, HALF)))


def banks_kernel(after, weights, numbers, bank, bank_last):
    build_level(bank, weights, numbers, 1)
    build_bank(bank_last, *level_params(weights, numbers, LEVELS - 1, slice(HALF, ROWS)))


def bank_and_part_kernel(level, trim, own, weights, numbers, bank, part):
    build_level(bank, weights, numbers, level)
    part[...] = fine_sum(child_product(bank.at[OUTS : 2 * OUTS], 0, own), trim)


def last_product(low, high, t, stack):
    at = slice(t * COLS, (t + 1) * COLS)
    bank = jnp.concatenate([low[:, at], high[:, at]], axis=0)
    rows = jnp.concatenate(child_rows_of(stack), axis=0)
    return jnp.dot(bank, rows, preferred_element_type=F32)


def parts_kernel(trim, own, low, high, parts):
    product = last_product(low, high, 0, own)
    for half in range(2):
        parts[half] = fine_sum(product[half * OUTS : (half + 1) * OUTS], trim)


def inside_mask(rows, length, rim):
    bins = lax.broadcasted_iota(jnp.int32, (rows, length), 1) + (lax.axis_index("range") * BINS - rim)
    return (bins >= 0) & (bins < (BINS * lax.axis_size("range")))


def takes_early(place):
    return place == lax.axis_size("range") // 2


def compress_kernel(sent, echoes, odd, late, early, toeplitz, out, window, rows=None):
    side = (lax.axis_index("aperture") & 1) ^ 1 if sent else lax.axis_index("aperture") & 1
    at = pl.multiple_of(side * HALF, HALF)
    is_odd = (lax.axis_index("range") & 1) == 1
    is_early = takes_early(lax.axis_index("range"))
    blocks = FRAME // LANES
    tiles = SPAN // LANES
    first = HALO // LANES
    last = first + BINS // LANES
    for part in range(2):
        for tile in range(blocks + tiles - 1):
            if first <= tile < last:
                spot = (tile - first) * LANES
                piece = echoes[part, pl.ds(at, HALF), spot : spot + LANES]
            else:
                spot = (tile if tile < first else tile - last) * LANES
                ours = jnp.where(
                    is_early,
                    early[part, pl.ds(at, HALF), spot : spot + LANES],
                    late[part, pl.ds(at, HALF), spot : spot + LANES],
                )
                other = odd[part, pl.ds(at, HALF), spot : spot + LANES]
                if tile < first:
                    piece = jnp.where(is_odd, ours, other)
                else:
                    piece = jnp.where(is_odd, other, ours)
            for block in range(max(0, tile - tiles + 1), min(blocks, tile + 1)):
                spot = part * SPAN + (tile - block) * LANES
                window[block * HALF : (block + 1) * HALF, spot : spot + LANES] = piece
    result = lax.dot_general(
        window[...], toeplitz[...], (((1,), (1,)), ((), ())), preferred_element_type=F32
    )
    position = lax.axis_index("range") * BINS - RIM
    target = out if sent else rows
    for block in range(blocks):
        bins = lax.broadcasted_iota(jnp.int32, (HALF, 2 * LANES), 1) & (LANES - 1)
        bins = bins + (position + block * LANES)
        inside = (bins >= 0) & (bins < BINS * lax.axis_size("range"))
        piece = jnp.where(inside, result[block * HALF : (block + 1) * HALF], 0.0).astype(BF16)
        at = slice(block * LANES, (block + 1) * LANES)
        for part in range(2):
            target[part * HALF : (part + 1) * HALF, at] = piece[:, part * LANES : (part + 1) * LANES]
    if not sent:
        fill_stack(out, rows[...])


def fill_stack(stack, source):
    length = source.shape[1]
    source = source.astype(F32)
    for a in range(COARSE):
        shift = (24 - 8 * a) % length
        moved = pltpu.roll(source, shift, 1) if shift else source
        stack[a * 32 : (a + 1) * 32] = moved.astype(BF16)


def fine_sum(product, trim):
    length = product.shape[1]
    total = None
    for b in range(FINE):
        piece = product[b * 32 : (b + 1) * 32]
        if b + trim:
            piece = pltpu.roll(piece, length - b - trim, 1)
        total = piece if total is None else total + piece
    return total


def rounded(total, rim):
    total = total[:, 0 : BINS + 2 * rim]
    return jnp.where(inside_mask(*total.shape, rim), total, 0.0).astype(BF16)


def merge_sent_kernel(trim, rim, own, theirs, bank, sent, partner):
    fill_stack(partner, theirs[...])
    product = both_products(bank.at[OUTS : 2 * OUTS], own, partner)
    sent[...] = rounded(fine_sum(product, trim), rim)


def merge_sent_part_kernel(trim, rim, part, theirs, bank, sent, partner):
    fill_stack(partner, theirs[...])
    product = child_product(bank.at[OUTS : 2 * OUTS], 1, partner)
    sent[...] = rounded(part[...] + fine_sum(product, trim), rim)


def merge_kept_kernel(trim, rim, own, partner, bank, after):
    product = both_products(bank.at[0:OUTS], own, partner)
    fill_stack(after, rounded(fine_sum(product, trim), rim))


def merge_last_kernel(parts, theirs, low, high, out, partner):
    fill_stack(partner, theirs[...])
    product = last_product(low, high, 1, partner)
    for half in range(2):
        total = parts[half] + fine_sum(product[half * OUTS : (half + 1) * OUTS], RIM_LATE)
        total = total[:, 0:BINS].astype(BF16)
        for part in range(2):
            out[part, half * HALF : (half + 1) * HALF] = total[part * HALF : (part + 1) * HALF]


WHOLE = pl.BlockSpec(memory_space=pltpu.VMEM)
PARAMS = pltpu.CompilerParams(vmem_limit_bytes=VMEM)
BANK = jax.ShapeDtypeStruct((2 * OUTS, 2 * COLS), BF16)
HALF_BANK = jax.ShapeDtypeStruct((OUTS, 2 * COLS), BF16)
FRAMES = (FRAME, FRAME, FRAME_LATE, FRAME_LATE)
RIMS = (RIM, RIM, RIM_LATE, RIM_LATE)


def message(length):
    return jax.ShapeDtypeStruct((2 * HALF, length), BF16)


def shifted(length):
    return jax.ShapeDtypeStruct((COLS // 2, length), BF16)


def small_cost():
    return pl.CostEstimate(flops=1000, bytes_accessed=1000, transcendentals=0)


def prepare(chirp, taps, numbers):
    return pl.pallas_call(
        prepare_kernel,
        out_shape=(
            jax.ShapeDtypeStruct((2 * LANES, 2 * SPAN), BF16),
            BANK,
            HALF_BANK,
            jax.ShapeDtypeStruct((ROWS, 4 * PART), F32),
            jax.ShapeDtypeStruct((ROWS, LANES), F32),
        ),
        in_specs=[WHOLE] * 3,
        out_specs=(WHOLE,) * 5,
        scratch_shapes=[pltpu.VMEM((ROWS, LANES), F32)],
        compiler_params=PARAMS,
        cost_estimate=pl.CostEstimate(flops=1_000_000_000, bytes_accessed=2_000_000, transcendentals=0),
        name="prepare",
    )(chirp, taps, numbers)


def make_banks(after, weights, numbers):
    return pl.pallas_call(
        banks_kernel,
        out_shape=(BANK, HALF_BANK),
        in_specs=[pl.BlockSpec(memory_space=pl.ANY), WHOLE, WHOLE],
        out_specs=(WHOLE, WHOLE),
        compiler_params=PARAMS,
        cost_estimate=small_cost(),
        name="banks",
    )(after, weights, numbers)


def bank_and_part(level, own, weights, numbers):
    return pl.pallas_call(
        functools.partial(bank_and_part_kernel, level, trim_of(level)),
        out_shape=(BANK, jax.ShapeDtypeStruct((2 * HALF, FRAMES[level]), F32)),
        in_specs=[WHOLE] * 3,
        out_specs=(WHOLE, WHOLE),
        compiler_params=PARAMS,
        cost_estimate=small_cost(),
        name=f"bank_and_part_{level}",
    )(own, weights, numbers)


def own_parts(level, own, low, high):
    return pl.pallas_call(
        functools.partial(parts_kernel, trim_of(level)),
        out_shape=jax.ShapeDtypeStruct((2, 2 * HALF, FRAMES[level]), F32),
        in_specs=[WHOLE] * 3,
        out_specs=WHOLE,
        compiler_params=PARAMS,
        cost_estimate=small_cost(),
        name=f"own_parts_{level}",
    )(own, low, high)


def trim_of(level):
    return RIMS[level] - RIMS[level + 1] if level + 1 < LEVELS else RIMS[level]


def compress(sent, echoes, odd, late, early, toeplitz):
    scratch = [pltpu.VMEM((FRAME // LANES * HALF, 2 * SPAN), BF16)]
    if not sent:
        scratch.append(pltpu.VMEM((2 * HALF, FRAME), BF16))
    return pl.pallas_call(
        functools.partial(compress_kernel, sent),
        out_shape=message(FRAME) if sent else shifted(FRAME),
        in_specs=[WHOLE] * 5,
        out_specs=WHOLE,
        scratch_shapes=scratch,
        compiler_params=PARAMS,
        cost_estimate=pl.CostEstimate(flops=200_000_000, bytes_accessed=1_000_000, transcendentals=0),
        name="compress_sent" if sent else "compress_kept",
    )(echoes, odd, late, early, toeplitz)


def merge_sent(level, own, theirs, bank, has_part=False):
    kernel = merge_sent_part_kernel if has_part else merge_sent_kernel
    return pl.pallas_call(
        functools.partial(kernel, trim_of(level), RIMS[level + 1]),
        out_shape=(message(FRAMES[level + 1]), shifted(FRAMES[level])),
        in_specs=[WHOLE] * 3,
        out_specs=(WHOLE, WHOLE),
        compiler_params=PARAMS,
        name=f"merge_{level}_sent",
    )(own, theirs, bank)


def merge_kept(level, own, partner, bank):
    return pl.pallas_call(
        functools.partial(merge_kept_kernel, trim_of(level), RIMS[level + 1]),
        out_shape=shifted(FRAMES[level + 1]),
        in_specs=[WHOLE] * 3,
        out_specs=WHOLE,
        compiler_params=PARAMS,
        cost_estimate=small_cost(),
        name=f"merge_{level}_kept",
    )(own, partner, bank)


def merge_last(parts, theirs, low, high):
    return pl.pallas_call(
        merge_last_kernel,
        out_shape=jax.ShapeDtypeStruct((2, ROWS, BINS), BF16),
        in_specs=[WHOLE] * 4,
        out_specs=WHOLE,
        scratch_shapes=[pltpu.VMEM((COLS // 2, FRAMES[LEVELS - 1]), BF16)],
        compiler_params=PARAMS,
        name="merge_last",
    )(parts, theirs, low, high)


def body(echoes, transmit_chirp, band_weights, band_offsets, band_widths, child_rows):
    count = lax.axis_size("range")
    is_odd = lax.axis_index("range") % 2 == 1
    head = echoes[:, :, :HALO]
    tail = echoes[:, :, BINS - HALO :]
    between = jnp.where(lax.axis_index("range") % 2 == 0, head, tail)
    within = jnp.where(is_odd, head, tail)
    within_late = jnp.where(lax.axis_index("range") % 2 != 1, tail, head)
    pairs = [(i, i + 1) for i in range(1, count - 1, 2)]
    early = lax.ppermute(within, "range", [(i ^ 1, i) for i in range(count) if takes_early(i)])
    odd = lax.ppermute(between, "range", pairs + [(j, i) for i, j in pairs])
    late = lax.ppermute(within_late, "range", [(i ^ 1, i) for i in range(count) if not takes_early(i)])
    taps = jnp.swapaxes(band_weights, 3, 4).reshape(LEVELS, PART, ROWS)
    numbers = jnp.concatenate([band_offsets, band_widths, child_rows[:, None]], axis=1)
    toeplitz, bank, low, weights, numbers = prepare(transmit_chirp, taps, numbers)
    sent = compress(True, echoes, odd, late, early, toeplitz)
    blocks = lax.axis_size("aperture")

    def trade(message, level):
        return lax.ppermute(message, "aperture", [(i, i ^ (1 << level)) for i in range(blocks)])

    theirs = trade(sent, 0)
    own = compress(False, echoes, odd, late, early, toeplitz)
    sent, partner = merge_sent(0, own, theirs, bank)
    theirs = trade(sent, 1)
    own = merge_kept(0, own, partner, bank)
    bank, high = make_banks(own, weights, numbers)
    sent, partner = merge_sent(1, own, theirs, bank)
    theirs = trade(sent, 2)
    own = merge_kept(1, own, partner, bank)
    bank, part = bank_and_part(2, own, weights, numbers)
    sent, partner = merge_sent(2, part, theirs, bank, True)
    theirs = trade(sent, 3)
    own = merge_kept(2, own, partner, bank)
    parts = own_parts(3, own, low, high)
    return merge_last(parts, theirs, low, high)


def solution(mesh):
    return jax.shard_map(
        body,
        mesh=mesh,
        in_specs=(
            P(None, "aperture", "range"),
            P(),
            P(None, None, None, "aperture", None),
            P(None, None, "aperture"),
            P(None, None, "aperture"),
            P(None, "aperture"),
        ),
        out_specs=P(None, "aperture", "range"),
        check_vma=False,
    )
```

```python
import functools

import jax
import jax.numpy as jnp
from jax import lax
from jax.experimental import pallas as pl
from jax.experimental.pallas import tpu as pltpu
from jax.sharding import PartitionSpec as P

KERN = 16
SHIFT = 16
LEVELS = 4
TAPS = 512
HALF = 16
ROWS = 32
LANES = 128
BINS = 1024
RIM = 128
FRAME = BINS + 2 * RIM
RIM_LATE = 64
FRAME_LATE = BINS + 2 * RIM_LATE
HALO = RIM + TAPS // 2
SPAN = LANES + TAPS
COARSE = 6
FINE = 8
COLS = 2 * COARSE * 32
OUTS = FINE * 32
PART = 64
VMEM = 48 * 1024 * 1024
BF16 = jnp.bfloat16
F32 = jnp.float32


def build_bank(bank, weights, numbers):
    lane = lax.broadcasted_iota(jnp.int32, (HALF, LANES), 1)
    imag = ((lane >> 4) & 1) == 1
    swapped = jnp.where(imag, pltpu.roll(weights, 16, 1), pltpu.roll(weights, LANES - 16, 1))
    sources = (jnp.where(imag, -weights, weights), swapped)
    column = [jnp.broadcast_to(number, (HALF, LANES)).astype(jnp.int32) for number in numbers]
    for t in range(2):
        width = jnp.where((lane & 15) == column[4], column[2 + t], 0)
        base = t * 32 + ((lane >> 4) & 1) * KERN
        for tile in range(2):
            coarse = (lane >> 5) if tile == 0 else 4 + ((lane >> 5) & 1)
            first = coarse * FINE - SHIFT - column[t]
            for b in range(FINE):
                tap = first + b
                live = (tap >= 0) & (tap < width)
                index = base | (tap & (KERN - 1))
                for part in range(2):
                    value = jnp.take_along_axis(
                        sources[part], index, axis=1, mode="promise_in_bounds"
                    )
                    value = jnp.where(live, value, 0.0)
                    high = value.astype(BF16).astype(F32)
                    rows = slice(b * 32 + part * HALF, b * 32 + (part + 1) * HALF)
                    at = t * COLS + tile * LANES
                    if tile == 0:
                        bank[rows, at : at + LANES] = high.astype(BF16)
                        bank[rows, at + 2 * LANES : at + 3 * LANES] = (value - high).astype(BF16)
                    else:
                        both = jnp.where(lane < LANES // 2, high, value - high)
                        bank[rows, at : at + LANES] = both.astype(BF16)


def child_rows_of(stack):
    return [stack[0:LANES], stack[LANES:], stack[LANES:], stack[0:LANES]]


def child_product(bank, t, stack):
    rows = jnp.concatenate(child_rows_of(stack), axis=0)
    return jnp.dot(bank[:, t * COLS : (t + 1) * COLS], rows, preferred_element_type=F32)


def both_products(bank, own, partner):
    rows = jnp.concatenate(child_rows_of(own) + child_rows_of(partner), axis=0)
    return jnp.dot(bank[...], rows, preferred_element_type=F32)


def level_params(weights, numbers, level, rows):
    swap = ((lax.axis_index("aperture") >> level) & 1) == 1
    tile = weights[rows, (level // 2) * LANES : (level // 2 + 1) * LANES]
    if level % 2:
        tile = pltpu.roll(tile, LANES - PART, 1)
    lane = lax.broadcasted_iota(jnp.int32, (HALF, LANES), 1)
    turned = jnp.where(lane < 32, pltpu.roll(tile, LANES - 32, 1), pltpu.roll(tile, 32, 1))
    own = numbers[rows, :]
    off, wide = 2 * level, 8 + 2 * level
    picks = [own[:, k : k + 1] for k in (off, off + 1, wide, wide + 1, 16 + level)]
    for k in (0, 2):
        pair = picks[k], picks[k + 1]
        picks[k] = jnp.where(swap, pair[1], pair[0])
        picks[k + 1] = jnp.where(swap, pair[0], pair[1])
    return jnp.where(swap, turned, tile), picks


def build_level(bank, weights, numbers, level):
    first = 0
    if level + 1 < LEVELS:
        first = (lax.axis_index("aperture") >> (level + 1)) & 1
    for half in range(2):
        side = half ^ first
        start = side * HALF if isinstance(side, int) else pl.multiple_of(side * HALF, HALF)
        build_bank(bank.at[half * OUTS : (half + 1) * OUTS], *level_params(weights, numbers, level, pl.ds(start, HALF)))


def prepare_kernel(
    chirp, taps_in, numbers_in, toeplitz, bank, bank_last, weights, numbers, table
):
    taps = chirp[...].astype(F32)
    taps = jnp.concatenate([taps, jnp.zeros((2, SPAN - TAPS), F32)], axis=1)
    real = pltpu.roll(jnp.broadcast_to(taps[0:1], (LANES, SPAN)), 0, 1, stride=1, stride_axis=0)
    imag = pltpu.roll(jnp.broadcast_to(taps[1:2], (LANES, SPAN)), 0, 1, stride=1, stride_axis=0)
    toeplitz[0:LANES, 0:SPAN] = real.astype(BF16)
    toeplitz[0:LANES, SPAN : 2 * SPAN] = imag.astype(BF16)
    toeplitz[LANES : 2 * LANES, 0:SPAN] = (-imag).astype(BF16)
    toeplitz[LANES : 2 * LANES, SPAN : 2 * SPAN] = real.astype(BF16)

    table[...] = jnp.zeros((ROWS, LANES), F32)
    for level in range(LEVELS):
        weights[:, level * PART : (level + 1) * PART] = taps_in[level].T
        own = numbers_in[level].astype(F32)
        table[2 * level : 2 * level + 2, 0:ROWS] = own[0:2]
        table[8 + 2 * level : 10 + 2 * level, 0:ROWS] = own[2:4]
        table[16 + level : 17 + level, 0:ROWS] = own[4:5]
    numbers[:, 0:ROWS] = table[...].T[0:ROWS]
    build_level(bank, weights, numbers, 0)
    build_bank(bank_last, *level_params(weights, numbers, LEVELS - 1, slice(0, HALF)))


def banks_kernel(after, weights, numbers, bank, bank_last):
    build_level(bank, weights, numbers, 1)
    build_bank(bank_last, *level_params(weights, numbers, LEVELS - 1, slice(HALF, ROWS)))


def bank_and_part_kernel(level, trim, own, weights, numbers, bank, part):
    build_level(bank, weights, numbers, level)
    part[...] = fine_sum(child_product(bank.at[OUTS : 2 * OUTS], 0, own), trim)


def last_product(low, high, t, stack):
    at = slice(t * COLS, (t + 1) * COLS)
    bank = jnp.concatenate([low[:, at], high[:, at]], axis=0)
    rows = jnp.concatenate(child_rows_of(stack), axis=0)
    return jnp.dot(bank, rows, preferred_element_type=F32)


def parts_kernel(trim, own, low, high, parts):
    product = last_product(low, high, 0, own)
    for half in range(2):
        parts[half] = fine_sum(product[half * OUTS : (half + 1) * OUTS], trim)


def inside_mask(rows, length, rim):
    bins = lax.broadcasted_iota(jnp.int32, (rows, length), 1) + (lax.axis_index("range") * BINS - rim)
    return (bins >= 0) & (bins < (BINS * lax.axis_size("range")))


def takes_early(place):
    return place == lax.axis_size("range") // 2


def compress_kernel(sent, echoes, odd, late, early, toeplitz, out, window, rows=None):
    side = (lax.axis_index("aperture") & 1) ^ 1 if sent else lax.axis_index("aperture") & 1
    at = pl.multiple_of(side * HALF, HALF)
    is_odd = (lax.axis_index("range") & 1) == 1
    is_early = takes_early(lax.axis_index("range"))
    blocks = FRAME // LANES
    tiles = SPAN // LANES
    first = HALO // LANES
    last = first + BINS // LANES
    for part in range(2):
        for tile in range(blocks + tiles - 1):
            if first <= tile < last:
                spot = (tile - first) * LANES
                piece = echoes[part, pl.ds(at, HALF), spot : spot + LANES]
            else:
                spot = (tile if tile < first else tile - last) * LANES
                ours = jnp.where(
                    is_early,
                    early[part, pl.ds(at, HALF), spot : spot + LANES],
                    late[part, pl.ds(at, HALF), spot : spot + LANES],
                )
                other = odd[part, pl.ds(at, HALF), spot : spot + LANES]
                if tile < first:
                    piece = jnp.where(is_odd, ours, other)
                else:
                    piece = jnp.where(is_odd, other, ours)
            for block in range(max(0, tile - tiles + 1), min(blocks, tile + 1)):
                spot = part * SPAN + (tile - block) * LANES
                window[block * HALF : (block + 1) * HALF, spot : spot + LANES] = piece
    result = lax.dot_general(
        window[...], toeplitz[...], (((1,), (1,)), ((), ())), preferred_element_type=F32
    )
    position = lax.axis_index("range") * BINS - RIM
    target = out if sent else rows
    for block in range(blocks):
        bins = lax.broadcasted_iota(jnp.int32, (HALF, 2 * LANES), 1) & (LANES - 1)
        bins = bins + (position + block * LANES)
        inside = (bins >= 0) & (bins < BINS * lax.axis_size("range"))
        piece = jnp.where(inside, result[block * HALF : (block + 1) * HALF], 0.0).astype(BF16)
        at = slice(block * LANES, (block + 1) * LANES)
        for part in range(2):
            target[part * HALF : (part + 1) * HALF, at] = piece[:, part * LANES : (part + 1) * LANES]
    if not sent:
        fill_stack(out, rows[...])


def fill_stack(stack, source):
    length = source.shape[1]
    source = source.astype(F32)
    for a in range(COARSE):
        shift = (24 - 8 * a) % length
        moved = pltpu.roll(source, shift, 1) if shift else source
        stack[a * 32 : (a + 1) * 32] = moved.astype(BF16)


def fine_sum(product, trim):
    length = product.shape[1]
    total = None
    for b in range(FINE):
        piece = product[b * 32 : (b + 1) * 32]
        if b + trim:
            piece = pltpu.roll(piece, length - b - trim, 1)
        total = piece if total is None else total + piece
    return total


def rounded(total, rim):
    total = total[:, 0 : BINS + 2 * rim]
    return jnp.where(inside_mask(*total.shape, rim), total, 0.0).astype(BF16)


def merge_sent_kernel(trim, rim, own, theirs, bank, sent, partner):
    fill_stack(partner, theirs[...])
    product = both_products(bank.at[OUTS : 2 * OUTS], own, partner)
    sent[...] = rounded(fine_sum(product, trim), rim)


def merge_sent_part_kernel(trim, rim, part, theirs, bank, sent, partner):
    fill_stack(partner, theirs[...])
    product = child_product(bank.at[OUTS : 2 * OUTS], 1, partner)
    sent[...] = rounded(part[...] + fine_sum(product, trim), rim)


def merge_kept_kernel(trim, rim, own, partner, bank, after):
    product = both_products(bank.at[0:OUTS], own, partner)
    fill_stack(after, rounded(fine_sum(product, trim), rim))


def merge_last_kernel(parts, theirs, low, high, out, partner, held, sems):
    fill_stack(partner, theirs[...])
    product = last_product(low, high, 1, partner)
    copies = []
    for half in range(2):
        total = parts[half] + fine_sum(product[half * OUTS : (half + 1) * OUTS], RIM_LATE)
        total = total[:, 0:BINS].astype(BF16)
        rows = slice(half * HALF, (half + 1) * HALF)
        for part in range(2):
            held[part, rows] = total[part * HALF : (part + 1) * HALF]
        copies.append(
            pltpu.make_async_copy(held.at[:, rows], out.at[:, rows], sems.at[half])
        )
        copies[half].start()
    for copy in copies:
        copy.wait()


WHOLE = pl.BlockSpec(memory_space=pltpu.VMEM)
PARAMS = pltpu.CompilerParams(vmem_limit_bytes=VMEM)
BANK = jax.ShapeDtypeStruct((2 * OUTS, 2 * COLS), BF16)
HALF_BANK = jax.ShapeDtypeStruct((OUTS, 2 * COLS), BF16)
FRAMES = (FRAME, FRAME, FRAME_LATE, FRAME_LATE)
RIMS = (RIM, RIM, RIM_LATE, RIM_LATE)


def message(length):
    return jax.ShapeDtypeStruct((2 * HALF, length), BF16)


def shifted(length):
    return jax.ShapeDtypeStruct((COLS // 2, length), BF16)


def small_cost():
    return pl.CostEstimate(flops=1000, bytes_accessed=1000, transcendentals=0)


def prepare(chirp, taps, numbers):
    return pl.pallas_call(
        prepare_kernel,
        out_shape=(
            jax.ShapeDtypeStruct((2 * LANES, 2 * SPAN), BF16),
            BANK,
            HALF_BANK,
            jax.ShapeDtypeStruct((ROWS, 4 * PART), F32),
            jax.ShapeDtypeStruct((ROWS, LANES), F32),
        ),
        in_specs=[WHOLE] * 3,
        out_specs=(WHOLE,) * 5,
        scratch_shapes=[pltpu.VMEM((ROWS, LANES), F32)],
        compiler_params=PARAMS,
        cost_estimate=pl.CostEstimate(flops=1_000_000_000, bytes_accessed=2_000_000, transcendentals=0),
        name="prepare",
    )(chirp, taps, numbers)


def make_banks(after, weights, numbers):
    return pl.pallas_call(
        banks_kernel,
        out_shape=(BANK, HALF_BANK),
        in_specs=[pl.BlockSpec(memory_space=pl.ANY), WHOLE, WHOLE],
        out_specs=(WHOLE, WHOLE),
        compiler_params=PARAMS,
        cost_estimate=small_cost(),
        name="banks",
    )(after, weights, numbers)


def bank_and_part(level, own, weights, numbers):
    return pl.pallas_call(
        functools.partial(bank_and_part_kernel, level, trim_of(level)),
        out_shape=(BANK, jax.ShapeDtypeStruct((2 * HALF, FRAMES[level]), F32)),
        in_specs=[WHOLE] * 3,
        out_specs=(WHOLE, WHOLE),
        compiler_params=PARAMS,
        cost_estimate=small_cost(),
        name=f"bank_and_part_{level}",
    )(own, weights, numbers)


def own_parts(level, own, low, high):
    return pl.pallas_call(
        functools.partial(parts_kernel, trim_of(level)),
        out_shape=jax.ShapeDtypeStruct((2, 2 * HALF, FRAMES[level]), F32),
        in_specs=[WHOLE] * 3,
        out_specs=WHOLE,
        compiler_params=PARAMS,
        cost_estimate=small_cost(),
        name=f"own_parts_{level}",
    )(own, low, high)


def trim_of(level):
    return RIMS[level] - RIMS[level + 1] if level + 1 < LEVELS else RIMS[level]


def compress(sent, echoes, odd, late, early, toeplitz):
    scratch = [pltpu.VMEM((FRAME // LANES * HALF, 2 * SPAN), BF16)]
    if not sent:
        scratch.append(pltpu.VMEM((2 * HALF, FRAME), BF16))
    return pl.pallas_call(
        functools.partial(compress_kernel, sent),
        out_shape=message(FRAME) if sent else shifted(FRAME),
        in_specs=[WHOLE] * 5,
        out_specs=WHOLE,
        scratch_shapes=scratch,
        compiler_params=PARAMS,
        cost_estimate=pl.CostEstimate(flops=200_000_000, bytes_accessed=1_000_000, transcendentals=0),
        name="compress_sent" if sent else "compress_kept",
    )(echoes, odd, late, early, toeplitz)


def merge_sent(level, own, theirs, bank, has_part=False):
    kernel = merge_sent_part_kernel if has_part else merge_sent_kernel
    return pl.pallas_call(
        functools.partial(kernel, trim_of(level), RIMS[level + 1]),
        out_shape=(message(FRAMES[level + 1]), shifted(FRAMES[level])),
        in_specs=[WHOLE] * 3,
        out_specs=(WHOLE, WHOLE),
        compiler_params=PARAMS,
        name=f"merge_{level}_sent",
    )(own, theirs, bank)


def merge_kept(level, own, partner, bank):
    return pl.pallas_call(
        functools.partial(merge_kept_kernel, trim_of(level), RIMS[level + 1]),
        out_shape=shifted(FRAMES[level + 1]),
        in_specs=[WHOLE] * 3,
        out_specs=WHOLE,
        compiler_params=PARAMS,
        cost_estimate=small_cost(),
        name=f"merge_{level}_kept",
    )(own, partner, bank)


def merge_last(parts, theirs, low, high):
    return pl.pallas_call(
        merge_last_kernel,
        out_shape=jax.ShapeDtypeStruct((2, ROWS, BINS), BF16),
        in_specs=[WHOLE] * 4,
        out_specs=pl.BlockSpec(memory_space=pl.ANY),
        scratch_shapes=[
            pltpu.VMEM((COLS // 2, FRAMES[LEVELS - 1]), BF16),
            pltpu.VMEM((2, ROWS, BINS), BF16),
            pltpu.SemaphoreType.DMA((2,)),
        ],
        compiler_params=PARAMS,
        name="merge_last",
    )(parts, theirs, low, high)


def body(echoes, transmit_chirp, band_weights, band_offsets, band_widths, child_rows):
    count = lax.axis_size("range")
    is_odd = lax.axis_index("range") % 2 == 1
    head = echoes[:, :, :HALO]
    tail = echoes[:, :, BINS - HALO :]
    between = jnp.where(lax.axis_index("range") % 2 == 0, head, tail)
    within = jnp.where(is_odd, head, tail)
    within_late = jnp.where(lax.axis_index("range") % 2 != 1, tail, head)
    pairs = [(i, i + 1) for i in range(1, count - 1, 2)]
    early = lax.ppermute(within, "range", [(i ^ 1, i) for i in range(count) if takes_early(i)])
    odd = lax.ppermute(between, "range", pairs + [(j, i) for i, j in pairs])
    late = lax.ppermute(within_late, "range", [(i ^ 1, i) for i in range(count) if not takes_early(i)])
    taps = jnp.swapaxes(band_weights, 3, 4).reshape(LEVELS, PART, ROWS)
    numbers = jnp.concatenate([band_offsets, band_widths, child_rows[:, None]], axis=1)
    toeplitz, bank, low, weights, numbers = prepare(transmit_chirp, taps, numbers)
    sent = compress(True, echoes, odd, late, early, toeplitz)
    blocks = lax.axis_size("aperture")

    def trade(message, level):
        return lax.ppermute(message, "aperture", [(i, i ^ (1 << level)) for i in range(blocks)])

    theirs = trade(sent, 0)
    own = compress(False, echoes, odd, late, early, toeplitz)
    sent, partner = merge_sent(0, own, theirs, bank)
    theirs = trade(sent, 1)
    own = merge_kept(0, own, partner, bank)
    bank, high = make_banks(own, weights, numbers)
    sent, partner = merge_sent(1, own, theirs, bank)
    theirs = trade(sent, 2)
    own = merge_kept(1, own, partner, bank)
    bank, part = bank_and_part(2, own, weights, numbers)
    sent, partner = merge_sent(2, part, theirs, bank, True)
    theirs = trade(sent, 3)
    own = merge_kept(2, own, partner, bank)
    parts = own_parts(3, own, low, high)
    return merge_last(parts, theirs, low, high)


def solution(mesh):
    return jax.shard_map(
        body,
        mesh=mesh,
        in_specs=(
            P(None, "aperture", "range"),
            P(),
            P(None, None, None, "aperture", None),
            P(None, None, "aperture"),
            P(None, None, "aperture"),
            P(None, "aperture"),
        ),
        out_specs=P(None, "aperture", "range"),
        check_vma=False,
    )
```
